512 devices in a mesh: seq: 64 (over y, z), fsdp: 8 (over x, core).
Axes of the slice: x: 4, y: 4, z: 16, core: 2. Of those that a mesh axis runs over, the one named last changes fastest.
Arguments:
- hidden: bfloat16 [8, 8192, 5120], P('fsdp', 'seq'), may hold values from -6 to 6
- inputs: bfloat16 [8, 8192, 2048], P('fsdp', 'seq'), may hold values from -6 to 6
- w_b: bfloat16 [5120, 128], P('fsdp'), may hold values from -0.078125 to 0.078125
- conv_x: float32 [4, 2048], replicated, may hold values from -3 to 3
- conv_b: float32 [4, 128], replicated, may hold values from -3 to 3
- log_decay: float32 [8, 8192, 64], P('fsdp', 'seq'), may hold values from -3.5 to 0, as said below
- accepted: int32 [8, 64], P('fsdp', 'seq'), may hold values from 0 to 128, as said below
Outputs:
- accepted_states: float32 [8, 64, 64, 32, 128], P('fsdp', 'seq')
The draws below stay inside these ranges and needn't reach their ends.
Inputs may be any that keep to these rules, and one draw needn't show every extreme that they name: `log_decay`: every entry is negative. `accepted`: in every context some shard keeps all 128 tokens.
All inputs are finite; a program needn't handle non-finite values.
Results may differ from the reference program's by a relative error of at most 0.0003.
Values may be sent and summed in bfloat16 or wider, within the bound.
No kernel may reach another device: no remote copies, remote signals or barrier semaphores. Data moves between devices by JAX's collectives and lax.ppermute only.
A program may use at most 192 MiB of HBM per device.

```python
import math
import jax
import jax.numpy as jnp
from jax import lax

D = 5120
HEADS = 64
HEADDIM = 32
STATE = 128
KW = 4
TOK_DEV = 128
CONTEXT_COUNT = 8
CONTEXT_LENGTH = 8192
N_SEQ = 64


def draw_log_decay(key, part):
    key = jax.random.fold_in(key, 11)
    sequence_flows = jax.random.split(key, 10)
    portion = 0.5
    lower_end = 0.5
    upper_end = 1.5
    lasting = jax.random.uniform(sequence_flows[0], (HEADS,)) < portion
    slow_rate = jax.random.uniform(sequence_flows[1], (HEADS,), minval=0.05, maxval=0.15) / CONTEXT_LENGTH
    fast_rate = jnp.exp(jax.random.uniform(sequence_flows[2], (HEADS,), minval=math.log(1.0 / 40.0), maxval=math.log(1.0 / 12.0)))
    per_step = jnp.where(lasting, slow_rate, fast_rate)
    shard_scale = jnp.exp(jax.random.uniform(sequence_flows[3], (CONTEXT_COUNT, N_SEQ, 1, 1), minval=math.log(0.01), maxval=math.log(2.0)))
    jitter = jax.random.uniform(sequence_flows[4], (CONTEXT_COUNT, N_SEQ, TOK_DEV, HEADS), minval=lower_end, maxval=upper_end)
    constant_rate = -(per_step * shard_scale * jitter).reshape(CONTEXT_COUNT, CONTEXT_LENGTH, HEADS)
    spike_position = jax.random.randint(sequence_flows[5], (CONTEXT_COUNT, 2), 0, CONTEXT_LENGTH)
    spike_length = jax.random.uniform(sequence_flows[6], (CONTEXT_COUNT, 2), minval=0.22, maxval=0.69)
    flagged_rows = jnp.arange(CONTEXT_LENGTH)[None, :, None] == spike_position[:, None, :]
    spike_runs = jnp.sum(jnp.where(flagged_rows, spike_length[:, None, :], 0.0), axis=2)
    run_start = jax.random.randint(sequence_flows[7], (CONTEXT_COUNT, 4), 0, CONTEXT_LENGTH)
    run_length = jax.random.randint(sequence_flows[8], (CONTEXT_COUNT, 4), 8, 17)
    run_total = jax.random.uniform(sequence_flows[9], (CONTEXT_COUNT, 4), minval=6.0, maxval=13.0)
    positions = jnp.arange(CONTEXT_LENGTH)[None, :, None]
    inside_run = (positions >= run_start[:, None, :]) & (positions < (run_start + run_length)[:, None, :])
    per_token = run_total / run_length.astype(jnp.float32)
    run_depth = jnp.max(jnp.where(inside_run, per_token[:, None, :], 0.0), axis=2)
    return (constant_rate - spike_runs[:, :, None] - run_depth[:, :, None]).astype(jnp.float32)


def draw_accepted(key, part):
    key = jax.random.fold_in(key, 23)
    first_key, second_key = jax.random.split(key)
    counts = jax.random.randint(first_key, (CONTEXT_COUNT, N_SEQ), 0, TOK_DEV + 1)
    chosen = jax.random.randint(second_key, (CONTEXT_COUNT, 1), 0, N_SEQ)
    return jnp.where(jnp.arange(N_SEQ)[None, :] == chosen, TOK_DEV, counts).astype(jnp.int32)


def block_levels(stream_key, dims, cuts, least, top_value):
    def one(dim, blocks):
        heights = jax.random.uniform(jax.random.fold_in(jax.random.fold_in(stream_key, 6), dim), (blocks,), jnp.float32, least / len(cuts), top_value / len(cuts))
        return jnp.repeat(jnp.exp(heights), dims[dim] // blocks).reshape((-1,) + (1,) * (len(dims) - dim - 1))

    level = one(*cuts[0])
    for cut in cuts[1:]:
        level = level * one(*cut)
    return level


def noise(rng, dims, deviation, limit, pieces=(), kind=jnp.bfloat16):
    entries = jax.random.normal(rng, dims, jnp.float32) * deviation
    if len(pieces) > 0:
        entries = block_levels(rng, dims, pieces, -0.22, 0.18) * entries
    return jnp.clip(entries, min=-limit, max=limit).astype(kind)


def setup_inputs(seed: int = 0) -> dict:
    streams_of = jax.random.split(jax.random.key(seed), 8)
    hidden = noise(streams_of[0], (CONTEXT_COUNT, CONTEXT_LENGTH, D), 1.0, 6.0, ((0, 8), (1, 64)))
    inputs = noise(streams_of[1], (CONTEXT_COUNT, CONTEXT_LENGTH, HEADS * HEADDIM), 1.0, 6.0, ((0, 8), (1, 64)))
    w_b = noise(streams_of[2], (D, STATE), D ** -0.5, 0.078125, ((0, 8),))
    conv_x = noise(streams_of[3], (KW, HEADS * HEADDIM), 0.5, 3.0, (), jnp.float32)
    conv_b = noise(streams_of[4], (KW, STATE), 0.5, 3.0, (), jnp.float32)
    log_decay = draw_log_decay(jax.random.fold_in(streams_of[7], 71), 0)
    accepted = draw_accepted(jax.random.fold_in(streams_of[7], 71), 0)
    return {"hidden": hidden, "inputs": inputs, "w_b": w_b, "conv_x": conv_x, "conv_b": conv_b, "log_decay": log_decay, "accepted": accepted}


def conv_rows(extended, weight):
    kernel = weight.shape[0]
    length = extended.shape[0] - kernel + 1
    summed = jnp.zeros((length, extended.shape[1]), jnp.float32)
    for offset in range(kernel):
        summed = summed + weight[offset] * extended[offset:offset + length]
    return jax.nn.silu(summed)


def shard_states(mixed_x, mixed_b, log_step, accepted):
    length = log_step.shape[0]
    prefix = jnp.concatenate([jnp.zeros((1, log_step.shape[1]), jnp.float32), jnp.cumsum(log_step, axis=0)], 0)
    end_logs = prefix[length]
    chosen = (jnp.arange(length + 1) == accepted).astype(jnp.float32)
    kept_log = jnp.sum(chosen[:, None] * prefix, axis=0)
    after_log = prefix[1:]
    inside = (jnp.arange(length) < accepted)[:, None]
    weight_end = jnp.exp(end_logs[None, :] - after_log)
    weight_kept = jnp.where(inside, jnp.exp(jnp.where(inside, kept_log[None, :] - after_log, 0.0)), 0.0)
    scaled = jnp.stack([weight_end, weight_kept])[:, :, :, None] * mixed_x[None]
    states = jnp.einsum("kthp,tn->khpn", scaled, mixed_b, precision=lax.Precision.HIGHEST)
    return end_logs, kept_log, states[0], states[1]


def reference(hidden, inputs, w_b, conv_x, conv_b, log_decay, accepted):
    outputs = []
    margin = conv_x.shape[0] - 1
    for context in range(hidden.shape[0]):
        projected = jnp.dot(hidden[context], w_b, preferred_element_type=jnp.float32)
        padded_b = jnp.concatenate([jnp.zeros((margin, STATE), jnp.float32), projected], 0)
        mixed_b = conv_rows(padded_b, conv_b).reshape(N_SEQ, TOK_DEV, STATE)
        padded_x = jnp.concatenate([jnp.zeros((margin, HEADS * HEADDIM), jnp.float32), inputs[context].astype(jnp.float32)], 0)
        mixed_x = conv_rows(padded_x, conv_x).reshape(N_SEQ, TOK_DEV, HEADS, HEADDIM)
        steps_log = log_decay[context].reshape(N_SEQ, TOK_DEV, HEADS)
        end_logs, kept_log, full_state, kept_state = jax.vmap(shard_states)(mixed_x, mixed_b, steps_log, accepted[context])

        def advance(incoming, item):
            shard_end, shard_kept, shard_full, shard_part = item
            result = jnp.exp(shard_kept)[:, None, None] * incoming + shard_part
            following = jnp.exp(shard_end)[:, None, None] * incoming + shard_full
            return following, result

        start_state = jnp.zeros((HEADS, HEADDIM, STATE), jnp.float32)
        unused, states = lax.scan(advance, start_state, (end_logs, kept_log, full_state, kept_state))
        outputs.append(states)
    return jnp.stack(outputs)
```

```python
import functools

import jax
import jax.numpy as jnp
from jax import lax
from jax.experimental import pallas as pl
from jax.experimental.pallas import tpu as pltpu
from jax.sharding import PartitionSpec as P

GROUP = 4
ROWS = 16
TOP = 32760.0
FINE = 128.0
LOG_STEP = float(2**19)
VMEM = 48 * 1024 * 1024

call = functools.partial(
    pl.pallas_call, compiler_params=pltpu.CompilerParams(vmem_limit_bytes=VMEM)
)


def code_states(states):
    top = jnp.maximum(jnp.max(jnp.abs(states), axis=1), 1e-33)
    scale = jnp.ceil(jnp.log2(top) * FINE)
    codes = states * (TOP * jnp.exp2(scale * (-1.0 / FINE)))[:, None, :]
    codes = jnp.round(codes).astype(jnp.int32).astype(jnp.int16)
    return codes, scale.astype(jnp.int32).astype(jnp.int16)


def read_states(codes, scale):
    step = jnp.exp2(scale.astype(jnp.int32).astype(jnp.float32) * (1.0 / FINE)) * (1.0 / TOP)
    return codes.astype(jnp.int32).astype(jnp.float32) * step[:, None, :]


def code_logs(logs):
    whole = jnp.round(logs * -LOG_STEP).astype(jnp.int32)
    high = lax.shift_right_logical(whole, 15)
    return high.astype(jnp.int16), (whole - high * 32768).astype(jnp.int16)


def read_logs(high, low):
    whole = high.astype(jnp.int32) * 32768 + low.astype(jnp.int32)
    return whole.astype(jnp.float32) * (-1.0 / LOG_STEP)


def partial_kernel(place, hidden, tail, w0, w1, w2, w3, total):
    depth = w0.shape[0]
    main = jnp.zeros((hidden.shape[0], w0.shape[1]), jnp.float32)
    edge = jnp.zeros((tail.shape[0], w0.shape[1]), jnp.float32)
    for step, w in enumerate((w0, w1, w2, w3)):
        owner = place[1] ^ (2 * step)
        columns = pl.ds(pl.multiple_of(owner * depth, 128), depth)
        main += jnp.dot(hidden[:, columns], w[...], preferred_element_type=jnp.float32)
        edge += jnp.dot(tail[:, columns], w[...], preferred_element_type=jnp.float32)
    total[0:ROWS, :] = edge
    total[ROWS:, :] = main


def mixed_b_kernel(place, hidden, tail, w, taps, begun, mixed, extended):
    depth = w.shape[1]
    main = begun[ROWS:, :]
    edge = begun[0:ROWS, :]
    for step in range(GROUP):
        owner = place[1] ^ (2 * step + 1)
        columns = pl.ds(pl.multiple_of(owner * depth, 128), depth)
        main += jnp.dot(hidden[:, columns], w[step], preferred_element_type=jnp.float32)
        edge += jnp.dot(tail[:, columns], w[step], preferred_element_type=jnp.float32)
    extended[0:ROWS, :] = edge
    extended[ROWS:, :] = main
    kernel = taps.shape[0]
    length = mixed.shape[0]
    summed = jnp.zeros(mixed.shape, jnp.float32)
    for offset in range(kernel):
        first = ROWS - kernel + 1 + offset
        summed = summed + taps[offset : offset + 1, :] * extended[first : first + length, :]
    mixed[...] = summed * jax.nn.sigmoid(summed)


def split_lanes(wide):
    high = wide.astype(jnp.bfloat16)
    low = (wide - high.astype(jnp.float32)).astype(jnp.bfloat16)
    return jnp.concatenate([high, low], axis=1)


def mixed_x_kernel(values, tail, taps, weight_end, weight_kept, ends, kepts, extended):
    length = values.shape[0]
    kernel = taps.shape[0]
    extended[0:ROWS, :] = tail[...].astype(jnp.float32)
    extended[ROWS:, :] = values[...].astype(jnp.float32)
    summed = jnp.zeros(values.shape, jnp.float32)
    for offset in range(kernel):
        first = ROWS - kernel + 1 + offset
        summed = summed + taps[offset : offset + 1, :] * extended[first : first + length, :]
    mixed = (summed * jax.nn.sigmoid(summed)).T
    heads = weight_end.shape[0]
    mixed = mixed.reshape(heads, mixed.shape[0] // heads, length)
    for weight, out in ((weight_end, ends), (weight_kept, kepts)):
        out[...] = split_lanes((mixed * weight[...][:, None, :]).reshape(-1, length))


def state_of(sides, mixed_b):
    high = mixed_b.astype(jnp.bfloat16)
    low = (mixed_b - high.astype(jnp.float32)).astype(jnp.bfloat16)
    size = mixed_b.shape[1]
    right = jnp.concatenate(
        [
            jnp.concatenate([high, low], axis=1),
            jnp.concatenate([high, jnp.zeros_like(low)], axis=1),
        ],
        axis=0,
    )
    both = jnp.dot(sides, right, preferred_element_type=jnp.float32)
    return both[:, :size] + both[:, size:]


def own_state_kernel(place, ends, mixed_b, out):
    out[...] = state_of(ends[...], mixed_b[...])


def sent_state_kernel(headdim, place, ends, mixed_b, logs, out):
    state = state_of(ends[...], mixed_b[...])
    rows, size = state.shape
    heads = rows // headdim
    codes, scale = code_states(state.reshape(heads, headdim, size))
    out[0:rows, :] = codes.reshape(rows, size)
    out[rows : rows + heads, :] = scale
    high, low = code_logs(logs[...])
    out[rows + heads : rows + 2 * heads, :] = high
    out[rows + 2 * heads : rows + 3 * heads, :] = low


def kept_state_kernel(kepts, mixed_b, out):
    out[...] = state_of(kepts[...], mixed_b[...])


def group_kernel(headdim, place, own, own_logs, got1, got2, got3, prefix, decay, sent, held, logs):
    rows, size = own.shape
    heads = rows // headdim
    first = place[0]
    held[first] = own[...]
    logs[first] = own_logs[...]
    for step, got in ((1, got1), (2, got2), (3, got3)):
        shard = first ^ step
        state = read_states(
            got[0:rows, :].reshape(heads, headdim, size), got[rows : rows + heads, :]
        )
        held[shard] = state.reshape(rows, size)
        logs[shard] = read_logs(
            got[rows + heads : rows + 2 * heads, :], got[rows + 2 * heads : rows + 3 * heads, :]
        )
    carried = jnp.zeros((heads, headdim, size), jnp.float32)
    passed = jnp.zeros((heads, size), jnp.float32)
    for shard in range(GROUP):
        prefix[shard] = carried.reshape(rows, size)
        decay[shard] = jnp.exp(passed)
        step_log = logs[shard]
        state = held[shard].reshape(heads, headdim, size)
        carried = jnp.exp(step_log)[:, None, :] * carried + state
        passed = passed + step_log
    codes, scale = code_states(carried)
    high, low = code_logs(passed)
    rest = jnp.zeros((heads, ROWS - 3, size), jnp.int32)
    notes = jnp.concatenate(
        [a.astype(jnp.int32)[:, None, :] for a in (scale, high, low)] + [rest], axis=1
    )
    sent[:, 0:headdim, :] = codes
    sent[:, headdim : headdim + ROWS, :] = notes.astype(jnp.int16)


def scan_kernel(headdim, got, sent):
    groups, size = got.shape[0], got.shape[2]
    carried = jnp.zeros((1, headdim, size), jnp.float32)
    for group in range(groups):
        codes, scale = code_states(carried)
        sent[group, 0:headdim, :] = codes[0]
        sent[group, headdim : headdim + ROWS, :] = jnp.broadcast_to(
            scale.astype(jnp.int32), (ROWS, size)
        ).astype(jnp.int16)
        notes = got[group, headdim : headdim + ROWS, :].astype(jnp.int32)
        state = read_states(got[group, 0:headdim, :][None], notes[0:1])
        log = read_logs(notes[1:2], notes[2:3])
        carried = jnp.exp(log)[:, None, :] * carried + state


def group_incoming(headdim, got, prefix, decay):
    size = got.shape[2]
    notes = got[:, headdim : headdim + ROWS, :].astype(jnp.int32)
    state = read_states(got[:, 0:headdim, :], notes[:, 0, :])
    local = prefix[0].reshape(-1, headdim, size)
    return decay[0][:, None, :] * state + local


def own_incoming_kernel(headdim, place, got, prefix, decay, out):
    out[...] = group_incoming(headdim, got, prefix, decay).reshape(out.shape)


def sent_incoming_kernel(headdim, place, got, prefix, decay, out):
    incoming = group_incoming(headdim, got, prefix, decay)
    heads, headdim, size = incoming.shape
    codes, scale = code_states(incoming)
    out[0 : heads * headdim, :] = codes.reshape(heads * headdim, size)
    out[heads * headdim :, :] = scale


def final_kernel(headdim, place, own, got1, got2, got3, kept, part, out):
    rows, size = own.shape
    heads = rows // headdim

    def place_slice(step, incoming):
        slot = place[0] ^ step
        lines = pl.ds(pl.multiple_of(slot * rows, rows), rows)
        heads_here = pl.ds(pl.multiple_of(slot * heads, heads), heads)
        scaled = kept[heads_here, :][:, None, :] * incoming
        out[lines, :] = scaled.reshape(rows, size) + part[lines, :]

    place_slice(0, own[...].reshape(heads, headdim, size))
    for step, got in ((1, got1), (2, got2), (3, got3)):
        place_slice(
            step,
            read_states(got[0:rows, :].reshape(heads, headdim, size), got[rows : rows + heads, :]),
        )


def whole(shape):
    return pl.BlockSpec(shape, lambda *_: (0,) * len(shape))


def gridded(kernel, grid, in_specs, out_specs, out_shape, scratch=()):
    return call(
        kernel,
        grid_spec=pltpu.PrefetchScalarGridSpec(
            num_scalar_prefetch=1,
            grid=grid,
            in_specs=in_specs,
            out_specs=out_specs,
            scratch_shapes=scratch,
        ),
        out_shape=out_shape,
    )


def on_device(hidden, inputs, w_b, conv_x, conv_b, log_decay, accepted):
    tokens = hidden[0]
    values = inputs[0]
    length, width = tokens.shape
    channels = values.shape[1]
    margin = conv_x.shape[0] - 1
    head_count = log_decay.shape[2]
    headdim = channels // head_count
    size = w_b.shape[1]
    depth = w_b.shape[0]
    heads = head_count // GROUP
    rows = heads * headdim
    f32, bf16, i16 = jnp.float32, jnp.bfloat16, jnp.int16

    shards = lax.axis_size("seq")
    parts = lax.axis_size("fsdp")
    shard = lax.axis_index("seq")
    place = jnp.stack([shard % GROUP, lax.axis_index("fsdp")]).astype(jnp.int32)

    ends = jnp.concatenate([tokens[length - margin :], values[length - margin :]], 1)
    before = lax.ppermute(ends, "seq", [(i, i + 1) for i in range(shards - 1)])
    tail = jnp.pad(before, ((ROWS - margin, 0), (0, 0)))
    w_own = [w_b] + [
        lax.ppermute(w_b, "fsdp", [(i, i ^ (2 * step)) for i in range(parts)])
        for step in (1, 2, 3)
    ]
    w_other = lax.ppermute(jnp.stack(w_own), "fsdp", [(i, i ^ 1) for i in range(parts)])

    prefix = jnp.concatenate(
        [jnp.zeros((1, head_count), f32), jnp.cumsum(log_decay[0], axis=0)], 0
    )
    kept = accepted[0, 0]
    end_logs = prefix[length]
    chosen = (jnp.arange(length + 1) == kept).astype(f32)
    kept_log = jnp.sum(chosen[:, None] * prefix, axis=0)
    after = prefix[1:].T
    inside = (jnp.arange(length) < kept)[None, :]
    weight_end = jnp.exp(end_logs[:, None] - after)
    weight_kept = jnp.where(
        inside, jnp.exp(jnp.where(inside, kept_log[:, None] - after, 0.0)), 0.0
    )
    wide_logs = jnp.broadcast_to(end_logs[:, None], (head_count, size))
    wide_kept = jnp.broadcast_to(jnp.exp(kept_log)[:, None], (head_count, size))

    sides = jax.ShapeDtypeStruct((channels, 2 * length), bf16)
    ends_x, kepts_x = call(
        mixed_x_kernel,
        grid=(GROUP,),
        in_specs=[
            pl.BlockSpec((length, rows), lambda i: (0, i)),
            pl.BlockSpec((ROWS, rows), lambda i: (0, i)),
            pl.BlockSpec((margin + 1, rows), lambda i: (0, i)),
            pl.BlockSpec((heads, length), lambda i: (i, 0)),
            pl.BlockSpec((heads, length), lambda i: (i, 0)),
        ],
        out_specs=[pl.BlockSpec((rows, 2 * length), lambda i: (i, 0))] * 2,
        out_shape=[sides, sides],
        scratch_shapes=[pltpu.VMEM((ROWS + length, rows), f32)],
    )(values, tail[:, width:], conv_x, weight_end, weight_kept)

    begun = gridded(
        partial_kernel,
        (1,),
        [whole((length, width)), whole((ROWS, width))] + [whole((depth, size))] * GROUP,
        whole((ROWS + length, size)),
        jax.ShapeDtypeStruct((ROWS + length, size), f32),
    )(place, tokens, tail[:, :width], *w_own)
    mixed_b = gridded(
        mixed_b_kernel,
        (1,),
        [
            whole((length, width)),
            whole((ROWS, width)),
            whole((GROUP, depth, size)),
            whole((margin + 1, size)),
            whole((ROWS + length, size)),
        ],
        whole((length, size)),
        jax.ShapeDtypeStruct((length, size), f32),
        [pltpu.VMEM((ROWS + length, size), f32)],
    )(place, tokens, tail[:, :width], w_other, conv_b, begun)

    def slice_of(step):
        return lambda i, place: (place[0] ^ step, 0)

    pairs = [[(i, i ^ step) for i in range(shards)] for step in range(GROUP)]
    got = []
    for step in (2, 3, 1):
        sent = gridded(
            functools.partial(sent_state_kernel, headdim),
            (1,),
            [
                pl.BlockSpec((rows, 2 * length), slice_of(step)),
                whole((length, size)),
                pl.BlockSpec((heads, size), slice_of(step)),
            ],
            whole((rows + 3 * heads, size)),
            jax.ShapeDtypeStruct((rows + 3 * heads, size), i16),
        )(place, ends_x, mixed_b, wide_logs)
        got.append(lax.ppermute(sent, "seq", pairs[step]))
    got = [got[2], got[0], got[1]]
    own = gridded(
        own_state_kernel,
        (1,),
        [pl.BlockSpec((rows, 2 * length), slice_of(0)), whole((length, size))],
        whole((rows, size)),
        jax.ShapeDtypeStruct((rows, size), f32),
    )(place, ends_x, mixed_b)
    part = call(
        kept_state_kernel,
        grid=(GROUP,),
        in_specs=[pl.BlockSpec((rows, 2 * length), lambda i: (i, 0)), whole((length, size))],
        out_specs=pl.BlockSpec((rows, size), lambda i: (i, 0)),
        out_shape=jax.ShapeDtypeStruct((channels, size), f32),
    )(kepts_x, mixed_b)

    groups = shards // GROUP
    message = (heads, headdim + ROWS, size)
    prefix_states, prefix_decay, sent = gridded(
        functools.partial(group_kernel, headdim),
        (1,),
        [whole((rows, size)), pl.BlockSpec((heads, size), slice_of(0))]
        + [whole((rows + 3 * heads, size))] * 3,
        [whole((GROUP, rows, size)), whole((GROUP, heads, size)), whole(message)],
        [
            jax.ShapeDtypeStruct((GROUP, rows, size), f32),
            jax.ShapeDtypeStruct((GROUP, heads, size), f32),
            jax.ShapeDtypeStruct(message, i16),
        ],
        [pltpu.VMEM((GROUP, rows, size), f32), pltpu.VMEM((GROUP, heads, size), f32)],
    )(place, own, wide_logs, *got)
    members = [[g * GROUP + b for g in range(groups)] for b in range(GROUP)]
    totals = lax.all_to_all(sent, "seq", 0, 0, axis_index_groups=members)
    scanned = call(
        functools.partial(scan_kernel, headdim),
        out_shape=jax.ShapeDtypeStruct(message, i16),
    )(totals)
    carried = lax.all_to_all(scanned, "seq", 0, 0, axis_index_groups=members)

    def incoming(kernel, step, out_rows, kind):
        return gridded(
            functools.partial(kernel, headdim),
            (1,),
            [
                whole(message),
                pl.BlockSpec((1, rows, size), lambda i, place: (place[0] ^ step, 0, 0)),
                pl.BlockSpec((1, heads, size), lambda i, place: (place[0] ^ step, 0, 0)),
            ],
            whole((out_rows, size)),
            jax.ShapeDtypeStruct((out_rows, size), kind),
        )(place, carried, prefix_states, prefix_decay)

    back = []
    for step in (2, 3, 1):
        sent = incoming(sent_incoming_kernel, step, rows + heads, i16)
        back.append(lax.ppermute(sent, "seq", pairs[step]))
    back = [back[2], back[0], back[1]]
    own = incoming(own_incoming_kernel, 0, rows, f32)
    final = gridded(
        functools.partial(final_kernel, headdim),
        (1,),
        [whole((rows, size))]
        + [whole((rows + heads, size))] * 3
        + [whole((head_count, size)), whole((channels, size))],
        whole((channels, size)),
        jax.ShapeDtypeStruct((channels, size), f32),
    )(place, own, *back, wide_kept, part)
    return final.reshape(1, 1, head_count, headdim, size)


def solution(mesh):
    placed = (
        P("fsdp", "seq", None),
        P("fsdp", "seq", None),
        P("fsdp", None),
        P(),
        P(),
        P("fsdp", "seq", None),
        P("fsdp", "seq"),
    )
    return jax.shard_map(
        on_device,
        mesh=mesh,
        in_specs=placed,
        out_specs=P("fsdp", "seq", None, None, None),
        check_vma=False,
    )
```

```python
import functools

import jax
import jax.numpy as jnp
from jax import lax
from jax.experimental import pallas as pl
from jax.experimental.pallas import tpu as pltpu
from jax.sharding import PartitionSpec as P

ROWS = 16
GROUP = 4
TOP = 32760.0
FINE = 128.0
LOG_STEP = float(2**19)
VMEM = 12 * 1024 * 1024


def call(kernel, *args, out, scratch=(), far=()):
    places = [
        pltpu.SMEM if a.shape == (1,) else pltpu.HBM if i in far else pltpu.VMEM
        for i, a in enumerate(args)
    ]
    return pl.pallas_call(
        kernel,
        in_specs=[pl.BlockSpec(memory_space=place) for place in places],
        out_specs=jax.tree.map(lambda _: pl.BlockSpec(memory_space=pltpu.VMEM), out),
        out_shape=out,
        scratch_shapes=scratch,
        compiler_params=pltpu.CompilerParams(vmem_limit_bytes=VMEM),
    )(*args)


def scale_codes(top):
    return jnp.ceil(jnp.log2(jnp.maximum(top, 1e-33)) * FINE)


def up(scale):
    return TOP * jnp.exp2(scale * (-1.0 / FINE))


def down(scale):
    return jnp.exp2(scale * (1.0 / FINE)) * (1.0 / TOP)


def pack(high, low):
    return lax.shift_left(high, 16) | (low & 0xFFFF)


def high_of(words):
    return lax.shift_right_arithmetic(words, 16)


def low_of(words):
    return lax.shift_right_arithmetic(lax.shift_left(words, 16), 16)


def words_of(scaled):
    codes = jnp.round(scaled).astype(jnp.int32)
    half = codes.shape[-2] // 2
    return pack(codes[..., :half, :], codes[..., half:, :])


def codes_of(words):
    return jnp.concatenate([high_of(words), low_of(words)], axis=-2).astype(jnp.float32)


def code_logs(logs):
    whole = jnp.round(logs * -LOG_STEP).astype(jnp.int32)
    lane = lax.broadcasted_iota(jnp.int32, logs.shape, 1)
    high = lax.shift_right_logical(whole, 15)
    return jnp.where(lane < logs.shape[1] // 2, high, whole & 0x7FFF)


def read_logs(notes):
    lane = lax.broadcasted_iota(jnp.int32, notes.shape, 1)
    parts = (notes & 0xFFFF).astype(jnp.float32)
    high = jnp.sum(jnp.where(lane == 0, parts, 0.0), axis=1, keepdims=True)
    low = jnp.sum(jnp.where(lane == notes.shape[1] - 1, parts, 0.0), axis=1, keepdims=True)
    return (high * 32768.0 + low) * (-1.0 / LOG_STEP)


def moved(pairs, arrived):
    moves = [
        pltpu.make_async_copy(source, target, arrived.at[i])
        for i, (source, target) in enumerate(pairs)
    ]
    for move in moves:
        move.start()
    for move in moves:
        move.wait()


def copies_kernel(w, out, held, arrived):
    moved([(w, held)], arrived)
    moved([(held, out.at[copy]) for copy in range(out.shape[0])], arrived)


def copies(w, count):
    return pl.pallas_call(
        copies_kernel,
        in_specs=[pl.BlockSpec(memory_space=pltpu.HBM)],
        out_specs=pl.BlockSpec(memory_space=pltpu.HBM),
        out_shape=jax.ShapeDtypeStruct((count, *w.shape), w.dtype),
        scratch_shapes=[pltpu.VMEM(w.shape, w.dtype), pltpu.SemaphoreType.DMA((count,))],
        compiler_params=pltpu.CompilerParams(vmem_limit_bytes=VMEM),
    )(w)


def edge_kernel(tokens, values, out, last_tokens, last_values, arrived):
    lines = pl.ds(tokens.shape[0] - ROWS, ROWS)
    moved([(tokens.at[lines, :], last_tokens), (values.at[lines, :], last_values)], arrived)
    margin, width = out.shape[0], tokens.shape[1]
    out[:, :width] = last_tokens[...].astype(jnp.float32)[ROWS - margin :, :].astype(out.dtype)
    out[:, width:] = last_values[...].astype(jnp.float32)[ROWS - margin :, :].astype(out.dtype)


def columns_of(chip, core, depth):
    return pl.ds(pl.multiple_of((2 * chip + core) * depth, 128), depth)


def project(core, hidden, tail, w, main, edge):
    depth = w.shape[1]
    for chip in range(w.shape[0]):
        some = hidden[:, chip * depth : (chip + 1) * depth]
        main += jnp.dot(some, w[chip], preferred_element_type=jnp.float32)
        some = tail[:, columns_of(chip, core, depth)]
        edge += jnp.dot(some, w[chip], preferred_element_type=jnp.float32)
    return main, edge


def partial_kernel(core, hidden, tail, w, total, rest, held, arrived):
    chips, depth, size = w.shape
    moved(
        [
            (hidden.at[:, columns_of(chip, side, depth)], to.at[:, pl.ds(chip * depth, depth)])
            for side, to in ((core[0], held), (1 - core[0], rest))
            for chip in range(chips)
        ],
        arrived,
    )
    main = jnp.zeros((hidden.shape[0], size), jnp.float32)
    edge = jnp.zeros((tail.shape[0], size), jnp.float32)
    main, edge = project(core[0], held, tail, w, main, edge)
    total[0:ROWS, :] = edge
    total[ROWS:, :] = main


def split_lanes(wide):
    high = wide.astype(jnp.bfloat16)
    low = (wide - high.astype(jnp.float32)).astype(jnp.bfloat16)
    return jnp.concatenate([high, low], axis=1)


def three_parts(wide):
    parts = []
    for _ in range(3):
        parts.append(wide.astype(jnp.bfloat16))
        wide = wide - parts[-1].astype(jnp.float32)
    return parts


def logs_of(steps):
    head_count, length = steps.shape
    earlier = lax.broadcasted_iota(jnp.int32, (length, length), 0)
    token = lax.broadcasted_iota(jnp.int32, (length, length), 1)
    upto = jnp.where(earlier <= token, 1.0, 0.0).astype(jnp.bfloat16)
    after = jnp.zeros((head_count, length), jnp.float32)
    for part in reversed(three_parts(steps)):
        after += jnp.dot(part, upto, preferred_element_type=jnp.float32)
    return after, lax.broadcasted_iota(jnp.int32, (head_count, length), 1)


def mixed_inputs(values, edge, taps, extended):
    length, channels = values.shape
    margin = taps.shape[0] - 1
    width = channels // GROUP
    extended[ROWS - margin : ROWS, :] = edge
    extended[ROWS:, :] = values[...].astype(jnp.float32)
    for part in range(GROUP):
        lanes = slice(part * width, (part + 1) * width)
        summed = jnp.zeros((length, width), jnp.float32)
        for offset in range(margin + 1):
            first = ROWS - margin + offset
            summed = (
                summed + taps[offset : offset + 1, lanes] * extended[first : first + length, lanes]
            )
        yield part, (summed * jax.nn.sigmoid(summed)).T


def weighted(mixed, weight):
    heads, length = weight.shape
    mixed = mixed.reshape(heads, mixed.shape[0] // heads, length)
    return split_lanes((mixed * weight[:, None, :]).reshape(-1, length))


def inputs_kernel(
    steps, values, before, taps, ends, end_logs, tail, extended, held, steps_held, taps_held, arrived
):
    moved([(values, held), (steps, steps_held), (taps, taps_held)], arrived)
    margin = taps.shape[0] - 1
    width = tail.shape[1]
    edge = before[...].astype(jnp.float32)
    zeros = jnp.zeros((ROWS - margin, width), jnp.float32)
    tail[...] = jnp.concatenate([zeros, edge[:, :width]], axis=0).astype(jnp.bfloat16)
    after, token = logs_of(steps_held[...])
    end_log = jnp.sum(jnp.where(token == token.shape[1] - 1, after, 0.0), axis=1, keepdims=True)
    weight = jnp.exp(end_log - after)
    end_logs[...] = jnp.broadcast_to(end_log, end_logs.shape)
    heads = weight.shape[0] // GROUP
    for part, mixed in mixed_inputs(held, edge[:, width:], taps_held, extended):
        rows = mixed.shape[0]
        some = weight[part * heads : (part + 1) * heads, :]
        ends[part * rows : (part + 1) * rows, :] = weighted(mixed, some)


def right_side(mixed_b):
    high = mixed_b.astype(jnp.bfloat16)
    low = (mixed_b - high.astype(jnp.float32)).astype(jnp.bfloat16)
    return jnp.concatenate(
        [
            jnp.concatenate([high, low], axis=1),
            jnp.concatenate([high, jnp.zeros_like(low)], axis=1),
        ],
        axis=0,
    )


def state_of(sides, right):
    both = jnp.dot(sides, right, preferred_element_type=jnp.float32)
    size = both.shape[1] // 2
    return both[:, :size] + both[:, size:]


def write_slice(sent, states, logs=None):
    heads, headdim, size = states.shape
    rows = heads * headdim // 2
    scale = scale_codes(jnp.max(jnp.abs(states), axis=1))
    sent[0:rows, :] = words_of(states * up(scale)[:, None, :]).reshape(rows, size)
    notes = scale.astype(jnp.int32)
    sent[rows:, :] = pack(notes, jnp.zeros_like(notes) if logs is None else code_logs(logs))


def read_slice(got, headdim):
    size = got.shape[1]
    half = headdim // 2
    heads = got.shape[0] // (half + 1)
    rows = heads * half
    notes = got[rows:, :]
    states = codes_of(got[0:rows, :].reshape(heads, half, size))
    return states * down(high_of(notes).astype(jnp.float32))[:, None, :], notes


def full_kernel(headdim, core, hidden, tail, w, taps, begun, ends, logs, sent, sides, extended):
    main, edge = project(1 - core[0], hidden, tail, w, begun[ROWS:, :], begun[0:ROWS, :])
    extended[0:ROWS, :] = edge
    extended[ROWS:, :] = main
    kernel = taps.shape[0]
    length, size = main.shape
    summed = jnp.zeros((length, size), jnp.float32)
    for offset in range(kernel):
        first = ROWS - kernel + 1 + offset
        summed = summed + taps[offset : offset + 1, :] * extended[first : first + length, :]
    right = right_side(summed * jax.nn.sigmoid(summed))
    sides[...] = right
    rows = ends.shape[0] // GROUP
    heads = rows // headdim
    for owner in range(GROUP):
        state = state_of(ends[owner * rows : (owner + 1) * rows, :], right)
        write_slice(
            sent.at[owner],
            state.reshape(heads, headdim, size),
            logs[owner * heads : (owner + 1) * heads, :],
        )


def kept_kernel(
    accepted, steps, values, before, taps, right, out, decay, extended, held, steps_held, taps_held, arrived
):
    moved([(values, held), (steps, steps_held), (taps, taps_held)], arrived)
    kept = accepted[0]
    after, token = logs_of(steps_held[...])
    kept_log = jnp.sum(jnp.where(token == kept - 1, after, 0.0), axis=1, keepdims=True)
    inside = token < kept
    weight = jnp.where(inside, jnp.exp(jnp.where(inside, kept_log - after, 0.0)), 0.0)
    decay[...] = jnp.broadcast_to(jnp.exp(kept_log), decay.shape)
    edge = before[...].astype(jnp.float32)[:, before.shape[1] - values.shape[1] :]
    heads = weight.shape[0] // GROUP
    for part, mixed in mixed_inputs(held, edge, taps_held, extended):
        rows = mixed.shape[0]
        some = weight[part * heads : (part + 1) * heads, :]
        out[part * rows : (part + 1) * rows, :] = state_of(weighted(mixed, some), right[...])


def group_kernel(headdim, got, prefix, decay, sent):
    rows, size = prefix.shape[1:]
    heads = rows // headdim
    half = headdim // 2
    message = half + 1
    carried = jnp.zeros((heads, headdim, size), jnp.float32)
    passed = jnp.zeros((heads, size), jnp.float32)
    for shard in range(GROUP):
        prefix[shard] = carried.reshape(rows, size)
        decay[shard] = jnp.exp(passed)
        state, notes = read_slice(got.at[shard], headdim)
        log = jnp.broadcast_to(read_logs(notes), (heads, size))
        carried = jnp.exp(log)[:, None, :] * carried + state
        passed = passed + log
    scale = scale_codes(jnp.max(jnp.abs(carried), axis=1))
    words = words_of(carried * up(scale)[:, None, :])
    for head in range(heads):
        sent[head * message : head * message + half, :] = words[head]
    sent[pl.ds(half, heads, stride=message), :] = pack(scale.astype(jnp.int32), code_logs(passed))


def scan_kernel(headdim, got, sent, held, tops, factors, decays):
    half = headdim // 2
    message = half + 1
    groups = got.shape[0] // message
    size = got.shape[1]
    notes = got[pl.ds(half, groups, stride=message), :]
    factors[...] = down(high_of(notes).astype(jnp.float32))
    decays[...] = jnp.broadcast_to(jnp.exp(read_logs(notes)), decays.shape)
    carried = jnp.zeros((headdim, size), jnp.float32)
    for group in range(groups):
        held[group * headdim : (group + 1) * headdim, :] = carried
        tops[group : group + 1, :] = jnp.max(jnp.abs(carried), axis=0, keepdims=True)
        state = codes_of(got[group * message : group * message + half, :])
        state = state * factors[group : group + 1, :]
        carried = decays[group : group + 1, :] * carried + state
    scale = scale_codes(tops[...])
    sent[pl.ds(half, groups, stride=message), :] = lax.shift_left(scale.astype(jnp.int32), 16)
    factors[...] = up(scale)
    for group in range(groups):
        scaled = held[group * headdim : (group + 1) * headdim, :] * factors[group : group + 1, :]
        sent[group * message : group * message + half, :] = words_of(scaled)


def incoming_kernel(headdim, got, prefix, decay, sent, held, factors):
    shards, rows, size = prefix.shape
    heads = rows // headdim
    half = headdim // 2
    message = half + 1
    notes = got[pl.ds(half, heads, stride=message), :]
    factors[...] = down(high_of(notes).astype(jnp.float32))
    for head in range(heads):
        state = codes_of(got[head * message : head * message + half, :])
        held[head] = state * factors[head : head + 1, :]
    for shard in range(shards):
        local = prefix[shard].reshape(heads, headdim, size)
        write_slice(sent.at[shard], decay[shard][:, None, :] * held[...] + local)


def final_kernel(headdim, got, kept, part, out):
    rows = part.shape[0] // GROUP
    size = part.shape[1]
    heads = rows // headdim
    for owner in range(GROUP):
        state, _ = read_slice(got.at[owner], headdim)
        scaled = kept[owner * heads : (owner + 1) * heads, :][:, None, :] * state
        lines = slice(owner * rows, (owner + 1) * rows)
        out[lines, :] = scaled.reshape(rows, size) + part[lines, :]


def on_device(hidden, inputs, w_b, conv_x, conv_b, log_decay, accepted):
    tokens = hidden[0]
    values = inputs[0]
    length, width = tokens.shape
    channels = values.shape[1]
    margin = conv_x.shape[0] - 1
    head_count = log_decay.shape[2]
    headdim = channels // head_count
    size = w_b.shape[1]
    message = headdim // 2 + 1
    heads = head_count // GROUP
    rows = heads * headdim
    f32, bf16, i32 = jnp.float32, jnp.bfloat16, jnp.int32
    array = jax.ShapeDtypeStruct
    shards = lax.axis_size("seq")
    parts = lax.axis_size("fsdp")
    group_count = shards // GROUP
    near = [[g * GROUP + i for i in range(GROUP)] for g in range(group_count)]
    far = [[g * GROUP + i for g in range(group_count)] for i in range(GROUP)]
    core = jnp.reshape(lax.axis_index("fsdp") % 2, (1,)).astype(i32)

    def exchange(sent, members):
        return lax.all_to_all(sent, "seq", 0, 0, axis_index_groups=members)

    def exchange_heads(sent):
        return exchange(sent.reshape(heads, 1, message * size), far).reshape(sent.shape)

    chips = [[i for i in range(parts) if i % 2 == c] for c in range(2)]
    w_copies = copies(w_b, parts // 2)
    w_own = lax.all_to_all(w_copies, "fsdp", 0, 0, axis_index_groups=chips)
    dma = pltpu.SemaphoreType.DMA
    edge = call(
        edge_kernel,
        tokens,
        values,
        far=(0, 1),
        out=array((margin, width + channels), bf16),
        scratch=[pltpu.VMEM((ROWS, width), bf16), pltpu.VMEM((ROWS, channels), bf16), dma((2,))],
    )
    before = lax.ppermute(edge, "seq", [(i, i + 1) for i in range(shards - 1)])

    steps = log_decay[0].T
    wide = array((head_count, size), f32)
    scratch = [
        pltpu.VMEM((ROWS + length, channels), f32),
        pltpu.VMEM(values.shape, values.dtype),
        pltpu.VMEM(steps.shape, f32),
        pltpu.VMEM(conv_x.shape, f32),
        dma((3,)),
    ]
    ends_x, end_logs, tail = call(
        inputs_kernel,
        steps,
        values,
        before,
        conv_x,
        far=(0, 1, 3),
        out=[array((channels, 2 * length), bf16), wide, array((ROWS, width), bf16)],
        scratch=scratch,
    )

    w_own, before = lax.optimization_barrier((w_own, before))
    w_other = lax.ppermute(w_own, "fsdp", [(i, i ^ 1) for i in range(parts)])
    begun, rest = call(
        partial_kernel,
        core,
        tokens,
        tail,
        w_own,
        far=(1,),
        out=[array((ROWS + length, size), f32), array((length, width // 2), bf16)],
        scratch=[pltpu.VMEM((length, width // 2), bf16), dma((parts,))],
    )

    slices = array((GROUP, heads * message, size), i32)
    sent, right = call(
        functools.partial(full_kernel, headdim),
        core,
        rest,
        tail,
        w_other,
        conv_b,
        begun,
        ends_x,
        end_logs,
        out=[slices, array((2 * length, 2 * size), bf16)],
        scratch=[pltpu.VMEM((ROWS + length, size), f32)],
    )
    prefix, decay, sent = call(
        functools.partial(group_kernel, headdim),
        exchange(sent, near),
        out=[
            array((GROUP, rows, size), f32),
            array((GROUP, heads, size), f32),
            array((heads * message, size), i32),
        ],
    )
    part, kept_decay = call(
        kept_kernel,
        accepted[0],
        steps,
        values,
        before,
        conv_x,
        right,
        far=(1, 2, 4),
        out=[array((channels, size), f32), wide],
        scratch=scratch,
    )

    sent = call(
        functools.partial(scan_kernel, headdim),
        exchange_heads(sent),
        out=array(sent.shape, i32),
        scratch=[pltpu.VMEM((group_count * headdim, size), f32)]
        + [pltpu.VMEM((group_count, size), f32)] * 3,
    )
    sent = call(
        functools.partial(incoming_kernel, headdim),
        exchange_heads(sent),
        prefix,
        decay,
        out=slices,
        scratch=[pltpu.VMEM((heads, headdim, size), f32), pltpu.VMEM((heads, size), f32)],
    )
    final = call(
        functools.partial(final_kernel, headdim),
        exchange(sent, near),
        kept_decay,
        part,
        out=array((channels, size), f32),
    )
    return final.reshape(1, 1, head_count, headdim, size)


def solution(mesh):
    placed = (
        P("fsdp", "seq", None),
        P("fsdp", "seq", None),
        P("fsdp", None),
        P(),
        P(),
        P("fsdp", "seq", None),
        P("fsdp", "seq"),
    )
    return jax.shard_map(
        on_device,
        mesh=mesh,
        in_specs=placed,
        out_specs=P("fsdp", "seq", None, None, None),
        check_vma=False,
    )
```

```python
import functools

import jax
import jax.numpy as jnp
from jax import lax
from jax.experimental import pallas as pl
from jax.experimental.pallas import tpu as pltpu
from jax.sharding import PartitionSpec as P

ROWS = 16
GROUP = 4
SHIFT = 2
TOP = 32760.0
FINE = 128.0
LOG_STEP = float(2**19)
VMEM = 12 * 1024 * 1024


def call(kernel, *args, out, scratch=(), far=(), out_space=pltpu.VMEM):
    places = [
        pltpu.SMEM if a.shape == (1,) else pltpu.HBM if i in far else pltpu.VMEM
        for i, a in enumerate(args)
    ]
    return pl.pallas_call(
        kernel,
        in_specs=[pl.BlockSpec(memory_space=place) for place in places],
        out_specs=jax.tree.map(lambda _: pl.BlockSpec(memory_space=out_space), out),
        out_shape=out,
        scratch_shapes=scratch,
        compiler_params=pltpu.CompilerParams(vmem_limit_bytes=VMEM),
    )(*args)


def scale_codes(top):
    return jnp.ceil(jnp.log2(jnp.maximum(top, 1e-33)) * FINE)


def up(scale):
    return TOP * jnp.exp2(scale * (-1.0 / FINE))


def down(scale):
    return jnp.exp2(scale * (1.0 / FINE)) * (1.0 / TOP)


def pack(high, low):
    return lax.shift_left(high, 16) | (low & 0xFFFF)


def high_of(words):
    return lax.shift_right_arithmetic(words, 16)


def low_of(words):
    return lax.shift_right_arithmetic(lax.shift_left(words, 16), 16)


def words_of(scaled):
    codes = jnp.round(scaled).astype(jnp.int32)
    half = codes.shape[-2] // 2
    return pack(codes[..., :half, :], codes[..., half:, :])


def codes_of(words):
    return jnp.concatenate([high_of(words), low_of(words)], axis=-2).astype(jnp.float32)


def code_logs(logs):
    whole = jnp.round(logs * -LOG_STEP).astype(jnp.int32)
    lane = lax.broadcasted_iota(jnp.int32, logs.shape, 1)
    high = lax.shift_right_logical(whole, 15)
    return jnp.where(lane < logs.shape[1] // 2, high, whole & 0x7FFF)


def read_logs(notes):
    lane = lax.broadcasted_iota(jnp.int32, notes.shape, 1)
    parts = (notes & 0xFFFF).astype(jnp.float32)
    high = jnp.sum(jnp.where(lane == 0, parts, 0.0), axis=1, keepdims=True)
    low = jnp.sum(jnp.where(lane == notes.shape[1] - 1, parts, 0.0), axis=1, keepdims=True)
    return (high * 32768.0 + low) * (-1.0 / LOG_STEP)


def moved(pairs, arrived):
    moves = [
        pltpu.make_async_copy(source, target, arrived.at[i])
        for i, (source, target) in enumerate(pairs)
    ]
    for move in moves:
        move.start()
    for move in moves:
        move.wait()


def copies_kernel(w, out, arrived):
    moved([(w, out.at[copy]) for copy in range(out.shape[0])], arrived)


def copies(w, count):
    return pl.pallas_call(
        copies_kernel,
        in_specs=[pl.BlockSpec(memory_space=pltpu.VMEM)],
        out_specs=pl.BlockSpec(memory_space=pltpu.HBM),
        out_shape=jax.ShapeDtypeStruct((count, *w.shape), w.dtype),
        scratch_shapes=[pltpu.SemaphoreType.DMA((count,))],
        compiler_params=pltpu.CompilerParams(vmem_limit_bytes=VMEM),
    )(w)


def edge_kernel(tokens, values, out, last_tokens, last_values, arrived):
    lines = pl.ds(tokens.shape[0] - ROWS, ROWS)
    moved([(tokens.at[lines, :], last_tokens), (values.at[lines, :], last_values)], arrived)
    margin, width = out.shape[0], tokens.shape[1]
    out[:, :width] = last_tokens[...].astype(jnp.float32)[ROWS - margin :, :].astype(out.dtype)
    out[:, width:] = last_values[...].astype(jnp.float32)[ROWS - margin :, :].astype(out.dtype)


def columns_of(chip, core, depth):
    return pl.ds(pl.multiple_of((2 * chip + core) * depth, 128), depth)


def project(core, hidden, tail, w, main, edge):
    depth = w.shape[1]
    for chip in range(w.shape[0]):
        some = hidden[:, chip * depth : (chip + 1) * depth]
        main += jnp.dot(some, w[chip], preferred_element_type=jnp.float32)
        some = tail[:, columns_of(chip, core, depth)]
        edge += jnp.dot(some, w[chip], preferred_element_type=jnp.float32)
    return main, edge


def partial_kernel(core, hidden, tail, w, total, rest, held, arrived):
    chips, depth, size = w.shape
    moved(
        [
            (hidden.at[:, columns_of(chip, side, depth)], to.at[:, pl.ds(chip * depth, depth)])
            for side, to in ((core[0], held), (1 - core[0], rest))
            for chip in range(chips)
        ],
        arrived,
    )
    main = jnp.zeros((hidden.shape[0], size), jnp.float32)
    edge = jnp.zeros((tail.shape[0], size), jnp.float32)
    main, edge = project(core[0], held, tail, w, main, edge)
    total[0:ROWS, :] = edge
    total[ROWS:, :] = main


def split_lanes(wide):
    high = wide.astype(jnp.bfloat16)
    low = (wide - high.astype(jnp.float32)).astype(jnp.bfloat16)
    return jnp.concatenate([high, low], axis=1)


def three_parts(wide):
    parts = []
    for _ in range(3):
        parts.append(wide.astype(jnp.bfloat16))
        wide = wide - parts[-1].astype(jnp.float32)
    return parts


def logs_of(steps):
    head_count, length = steps.shape
    earlier = lax.broadcasted_iota(jnp.int32, (length, length), 0)
    token = lax.broadcasted_iota(jnp.int32, (length, length), 1)
    upto = jnp.where(earlier <= token, 1.0, 0.0).astype(jnp.bfloat16)
    after = jnp.zeros((head_count, length), jnp.float32)
    for part in reversed(three_parts(steps)):
        after += jnp.dot(part, upto, preferred_element_type=jnp.float32)
    return after, lax.broadcasted_iota(jnp.int32, (head_count, length), 1)


def mixed_inputs(values, edge, taps, extended):
    length, channels = values.shape
    margin = taps.shape[0] - 1
    width = channels // GROUP
    extended[ROWS - margin : ROWS, :] = edge
    extended[ROWS:, :] = values[...].astype(jnp.float32)
    for part in range(GROUP):
        lanes = slice(part * width, (part + 1) * width)
        summed = jnp.zeros((length, width), jnp.float32)
        for offset in range(margin + 1):
            first = ROWS - margin + offset
            summed = (
                summed + taps[offset : offset + 1, lanes] * extended[first : first + length, lanes]
            )
        yield part, (summed * jax.nn.sigmoid(summed)).T


def weighted(mixed, weight):
    heads, length = weight.shape
    mixed = mixed.reshape(heads, mixed.shape[0] // heads, length)
    return split_lanes((mixed * weight[:, None, :]).reshape(-1, length))


def inputs_kernel(
    steps, values, before, taps, ends, end_logs, tail, extended, held, steps_held, taps_held, arrived
):
    moved([(values, held), (steps, steps_held), (taps, taps_held)], arrived)
    margin = taps.shape[0] - 1
    width = tail.shape[1]
    edge = before[...].astype(jnp.float32)
    zeros = jnp.zeros((ROWS - margin, width), jnp.float32)
    tail[...] = jnp.concatenate([zeros, edge[:, :width]], axis=0).astype(jnp.bfloat16)
    after, token = logs_of(steps_held[...])
    end_log = jnp.sum(jnp.where(token == token.shape[1] - 1, after, 0.0), axis=1, keepdims=True)
    weight = jnp.exp(end_log - after)
    end_logs[...] = jnp.broadcast_to(end_log, end_logs.shape)
    heads = weight.shape[0] // GROUP
    for part, mixed in mixed_inputs(held, edge[:, width:], taps_held, extended):
        rows = mixed.shape[0]
        some = weight[part * heads : (part + 1) * heads, :]
        ends[part * rows : (part + 1) * rows, :] = weighted(mixed, some)


def right_side(mixed_b):
    high = mixed_b.astype(jnp.bfloat16)
    low = (mixed_b - high.astype(jnp.float32)).astype(jnp.bfloat16)
    return jnp.concatenate(
        [
            jnp.concatenate([high, low], axis=1),
            jnp.concatenate([high, jnp.zeros_like(low)], axis=1),
        ],
        axis=0,
    )


def state_of(sides, right):
    both = jnp.dot(sides, right, preferred_element_type=jnp.float32)
    size = both.shape[1] // 2
    return both[:, :size] + both[:, size:]


def write_slice(sent, states, logs=None):
    heads, headdim, size = states.shape
    rows = heads * headdim // 2
    scale = scale_codes(jnp.max(jnp.abs(states), axis=1))
    sent[0:rows, :] = words_of(states * up(scale)[:, None, :]).reshape(rows, size)
    notes = scale.astype(jnp.int32)
    sent[rows:, :] = pack(notes, jnp.zeros_like(notes) if logs is None else code_logs(logs))


def read_slice(got, headdim):
    size = got.shape[1]
    half = headdim // 2
    heads = got.shape[0] // (half + 1)
    rows = heads * half
    notes = got[rows:, :]
    states = codes_of(got[0:rows, :].reshape(heads, half, size))
    return states * down(high_of(notes).astype(jnp.float32))[:, None, :], notes


def full_kernel(headdim, core, hidden, tail, w, taps, begun, ends, logs, sent, sides, extended):
    main, edge = project(1 - core[0], hidden, tail, w, begun[ROWS:, :], begun[0:ROWS, :])
    extended[0:ROWS, :] = edge
    extended[ROWS:, :] = main
    kernel = taps.shape[0]
    length, size = main.shape
    summed = jnp.zeros((length, size), jnp.float32)
    for offset in range(kernel):
        first = ROWS - kernel + 1 + offset
        summed = summed + taps[offset : offset + 1, :] * extended[first : first + length, :]
    right = right_side(summed * jax.nn.sigmoid(summed))
    sides[...] = right
    rows = ends.shape[0] // GROUP
    heads = rows // headdim
    for owner in range(GROUP):
        state = state_of(ends[owner * rows : (owner + 1) * rows, :], right)
        write_slice(
            sent.at[owner],
            state.reshape(heads, headdim, size),
            logs[owner * heads : (owner + 1) * heads, :],
        )


def kept_kernel(
    accepted, steps, values, before, taps, right, out, decay, extended, held, steps_held, taps_held, arrived
):
    moved([(values, held), (steps, steps_held), (taps, taps_held)], arrived)
    kept = accepted[0]
    after, token = logs_of(steps_held[...])
    kept_log = jnp.sum(jnp.where(token == kept - 1, after, 0.0), axis=1, keepdims=True)
    inside = token < kept
    weight = jnp.where(inside, jnp.exp(jnp.where(inside, kept_log - after, 0.0)), 0.0)
    decay[...] = jnp.broadcast_to(jnp.exp(kept_log), decay.shape)
    edge = before[...].astype(jnp.float32)[:, before.shape[1] - values.shape[1] :]
    heads = weight.shape[0] // GROUP
    for part, mixed in mixed_inputs(held, edge, taps_held, extended):
        rows = mixed.shape[0]
        some = weight[part * heads : (part + 1) * heads, :]
        out[part * rows : (part + 1) * rows, :] = state_of(weighted(mixed, some), right[...])


def group_kernel(headdim, wraps, got, prefix, decay, sent):
    goes_on = jnp.where(wraps[0] > 0, 0.0, 1.0)
    rows, size = prefix.shape[1:]
    heads = rows // headdim
    half = headdim // 2
    message = half + 1
    carried = jnp.zeros((heads, headdim, size), jnp.float32)
    passed = jnp.zeros((heads, size), jnp.float32)
    for shard in range(GROUP):
        if shard == SHIFT:
            carried = carried * goes_on
            passed = passed * goes_on
        prefix[shard] = carried.reshape(rows, size)
        decay[shard] = jnp.exp(passed) * (goes_on if shard >= SHIFT else 1.0)
        state, notes = read_slice(got.at[shard], headdim)
        log = jnp.broadcast_to(read_logs(notes), (heads, size))
        carried = jnp.exp(log)[:, None, :] * carried + state
        passed = passed + log
    scale = scale_codes(jnp.max(jnp.abs(carried), axis=1))
    words = words_of(carried * up(scale)[:, None, :])
    for head in range(heads):
        sent[head * message : head * message + half, :] = words[head]
    sent[pl.ds(half, heads, stride=message), :] = pack(scale.astype(jnp.int32), code_logs(passed))


def scan_kernel(headdim, core, got, sent, held, tops, factors, decays):
    half = headdim // 2
    message = half + 1
    groups = got.shape[0] // message
    size = got.shape[1]
    notes = got[pl.ds(half, groups, stride=message), :]
    factors[...] = down(high_of(notes).astype(jnp.float32))
    decays[...] = jnp.broadcast_to(jnp.exp(read_logs(notes)), decays.shape)
    first = codes_of(got[(groups - 1) * message : (groups - 1) * message + half, :])
    carried = first * factors[groups - 1 : groups, :] * jnp.where(core[0] > 0, 1.0, 0.0)
    for group in range(groups):
        held[group * headdim : (group + 1) * headdim, :] = carried
        tops[group : group + 1, :] = jnp.max(jnp.abs(carried), axis=0, keepdims=True)
        state = codes_of(got[group * message : group * message + half, :])
        state = state * factors[group : group + 1, :]
        carried = decays[group : group + 1, :] * carried + state
    scale = scale_codes(tops[...])
    sent[pl.ds(half, groups, stride=message), :] = lax.shift_left(scale.astype(jnp.int32), 16)
    factors[...] = up(scale)
    for group in range(groups):
        scaled = held[group * headdim : (group + 1) * headdim, :] * factors[group : group + 1, :]
        sent[group * message : group * message + half, :] = words_of(scaled)


def incoming_kernel(headdim, got, prefix, decay, sent, held, factors, staged, arrived):
    shards, rows, size = prefix.shape
    heads = rows // headdim
    half = headdim // 2
    message = half + 1
    notes = got[pl.ds(half, heads, stride=message), :]
    factors[...] = down(high_of(notes).astype(jnp.float32))
    for head in range(heads):
        state = codes_of(got[head * message : head * message + half, :])
        held[head] = state * factors[head : head + 1, :]
    for shard in range(shards):
        local = prefix[shard].reshape(heads, headdim, size)
        write_slice(staged.at[shard], decay[shard][:, None, :] * held[...] + local)
        pltpu.make_async_copy(staged.at[shard], sent.at[shard], arrived.at[shard]).start()
    for shard in range(shards):
        pltpu.make_async_copy(staged.at[shard], sent.at[shard], arrived.at[shard]).wait()


def final_kernel(headdim, got, kept, part, out, staged, arrived):
    rows = part.shape[0] // GROUP
    size = part.shape[1]
    heads = rows // headdim
    moves = []
    for owner in range(GROUP):
        state, _ = read_slice(got.at[owner], headdim)
        scaled = kept[owner * heads : (owner + 1) * heads, :][:, None, :] * state
        lines = slice(owner * rows, (owner + 1) * rows)
        staged[lines, :] = scaled.reshape(rows, size) + part[lines, :]
        lines = pl.ds(owner * rows, rows)
        moves.append(
            pltpu.make_async_copy(staged.at[lines, :], out.at[lines, :], arrived.at[owner])
        )
        moves[-1].start()
    for move in moves:
        move.wait()


def on_device(hidden, inputs, w_b, conv_x, conv_b, log_decay, accepted):
    tokens = hidden[0]
    values = inputs[0]
    length, width = tokens.shape
    channels = values.shape[1]
    margin = conv_x.shape[0] - 1
    head_count = log_decay.shape[2]
    headdim = channels // head_count
    size = w_b.shape[1]
    message = headdim // 2 + 1
    heads = head_count // GROUP
    rows = heads * headdim
    f32, bf16, i32 = jnp.float32, jnp.bfloat16, jnp.int32
    array = jax.ShapeDtypeStruct
    shards = lax.axis_size("seq")
    parts = lax.axis_size("fsdp")
    group_count = shards // GROUP

    def device(side, part, place):
        return (place + SHIFT * side) % shards * parts + 2 * part + side

    sides = [(side, part) for part in range(parts // 2) for side in range(2)]
    near = [
        [device(side, part, group * GROUP + i) for i in range(GROUP)]
        for side, part in sides
        for group in range(group_count)
    ]
    far = [
        [device(side, part, group * GROUP + i) for group in range(group_count)]
        for side, part in sides
        for i in range(GROUP)
    ]
    core = lax.axis_index("fsdp") % 2
    place = (lax.axis_index("seq") - SHIFT * core) % shards
    wraps = jnp.reshape(core * (place // GROUP == group_count - 1), (1,)).astype(i32)
    core = jnp.reshape(core, (1,)).astype(i32)

    def exchange(sent, members):
        return lax.all_to_all(sent, ("seq", "fsdp"), 0, 0, axis_index_groups=members)

    def exchange_heads(sent):
        return exchange(sent.reshape(heads, 1, message * size), far).reshape(sent.shape)

    chips = [[i for i in range(parts) if i % 2 == c] for c in range(2)]
    w_copies = copies(w_b, parts // 2)
    w_own = lax.all_to_all(w_copies, "fsdp", 0, 0, axis_index_groups=chips)
    dma = pltpu.SemaphoreType.DMA
    edge = call(
        edge_kernel,
        tokens,
        values,
        far=(0, 1),
        out=array((margin, width + channels), bf16),
        scratch=[pltpu.VMEM((ROWS, width), bf16), pltpu.VMEM((ROWS, channels), bf16), dma((2,))],
    )
    before = lax.ppermute(edge, "seq", [(i, i + 1) for i in range(shards - 1)])

    steps = log_decay[0].T
    wide = array((head_count, size), f32)
    scratch = [
        pltpu.VMEM((ROWS + length, channels), f32),
        pltpu.VMEM(values.shape, values.dtype),
        pltpu.VMEM(steps.shape, f32),
        pltpu.VMEM(conv_x.shape, f32),
        dma((3,)),
    ]
    ends_x, end_logs, tail = call(
        inputs_kernel,
        steps,
        values,
        before,
        conv_x,
        far=(0, 1, 3),
        out=[array((channels, 2 * length), bf16), wide, array((ROWS, width), bf16)],
        scratch=scratch,
    )

    w_own, before = lax.optimization_barrier((w_own, before))
    w_other = lax.ppermute(w_own, "fsdp", [(i, i ^ 1) for i in range(parts)])
    begun, rest = call(
        partial_kernel,
        core,
        tokens,
        tail,
        w_own,
        far=(1,),
        out=[array((ROWS + length, size), f32), array((length, width // 2), bf16)],
        scratch=[pltpu.VMEM((length, width // 2), bf16), dma((parts,))],
    )

    slices = array((GROUP, heads * message, size), i32)
    sent, right = call(
        functools.partial(full_kernel, headdim),
        core,
        rest,
        tail,
        w_other,
        conv_b,
        begun,
        ends_x,
        end_logs,
        out=[slices, array((2 * length, 2 * size), bf16)],
        scratch=[pltpu.VMEM((ROWS + length, size), f32)],
    )
    prefix, decay, sent = call(
        functools.partial(group_kernel, headdim),
        wraps,
        exchange(sent, near),
        out=[
            array((GROUP, rows, size), f32),
            array((GROUP, heads, size), f32),
            array((heads * message, size), i32),
        ],
    )
    part, kept_decay = call(
        kept_kernel,
        accepted[0],
        steps,
        values,
        before,
        conv_x,
        right,
        far=(1, 2, 4),
        out=[array((channels, size), f32), wide],
        scratch=scratch,
    )

    sent = call(
        functools.partial(scan_kernel, headdim),
        core,
        exchange_heads(sent),
        out=array(sent.shape, i32),
        scratch=[pltpu.VMEM((group_count * headdim, size), f32)]
        + [pltpu.VMEM((group_count, size), f32)] * 3,
    )
    sent = call(
        functools.partial(incoming_kernel, headdim),
        exchange_heads(sent),
        prefix,
        decay,
        out=slices,
        out_space=pltpu.HBM,
        scratch=[
            pltpu.VMEM((heads, headdim, size), f32),
            pltpu.VMEM((heads, size), f32),
            pltpu.VMEM(slices.shape, i32),
            dma((GROUP,)),
        ],
    )
    final = call(
        functools.partial(final_kernel, headdim),
        exchange(sent, near),
        kept_decay,
        part,
        out=array((channels, size), f32),
        out_space=pltpu.HBM,
        scratch=[pltpu.VMEM((channels, size), f32), dma((GROUP,))],
    )
    return final.reshape(1, 1, head_count, headdim, size)


def solution(mesh):
    placed = (
        P("fsdp", "seq", None),
        P("fsdp", "seq", None),
        P("fsdp", None),
        P(),
        P(),
        P("fsdp", "seq", None),
        P("fsdp", "seq"),
    )
    return jax.shard_map(
        on_device,
        mesh=mesh,
        in_specs=placed,
        out_specs=P("fsdp", "seq", None, None, None),
        check_vma=False,
    )
```

```python
import functools

import jax
import jax.numpy as jnp
from jax import lax
from jax.experimental import pallas as pl
from jax.experimental.pallas import tpu as pltpu
from jax.sharding import PartitionSpec as P

ROWS = 16
GROUP = 4
SHIFT = 2
TOP = 32760.0
FINE = 128.0
LOG_STEP = float(2**19)
VMEM = 12 * 1024 * 1024


def call(kernel, *args, out, scratch=(), far=(), out_space=pltpu.VMEM):
    places = [
        pltpu.SMEM if a.shape == (1,) else pltpu.HBM if i in far else pltpu.VMEM
        for i, a in enumerate(args)
    ]
    return pl.pallas_call(
        kernel,
        in_specs=[pl.BlockSpec(memory_space=place) for place in places],
        out_specs=jax.tree.map(lambda _: pl.BlockSpec(memory_space=out_space), out),
        out_shape=out,
        scratch_shapes=scratch,
        compiler_params=pltpu.CompilerParams(vmem_limit_bytes=VMEM),
    )(*args)


def scale_codes(top):
    return jnp.ceil(jnp.log2(jnp.maximum(top, 1e-33)) * FINE)


def up(scale):
    return TOP * jnp.exp2(scale * (-1.0 / FINE))


def down(scale):
    return jnp.exp2(scale * (1.0 / FINE)) * (1.0 / TOP)


def pack(high, low):
    return lax.shift_left(high, 16) | (low & 0xFFFF)


def high_of(words):
    return lax.shift_right_arithmetic(words, 16)


def low_of(words):
    return lax.shift_right_arithmetic(lax.shift_left(words, 16), 16)


def words_of(scaled):
    codes = jnp.round(scaled).astype(jnp.int32)
    half = codes.shape[-2] // 2
    return pack(codes[..., :half, :], codes[..., half:, :])


def codes_of(words):
    return jnp.concatenate([high_of(words), low_of(words)], axis=-2).astype(jnp.float32)


def code_logs(logs):
    whole = jnp.round(logs * -LOG_STEP).astype(jnp.int32)
    lane = lax.broadcasted_iota(jnp.int32, logs.shape, 1)
    high = lax.shift_right_logical(whole, 15)
    return jnp.where(lane < logs.shape[1] // 2, high, whole & 0x7FFF)


def read_logs(notes):
    lane = lax.broadcasted_iota(jnp.int32, notes.shape, 1)
    parts = (notes & 0xFFFF).astype(jnp.float32)
    high = jnp.sum(jnp.where(lane == 0, parts, 0.0), axis=1, keepdims=True)
    low = jnp.sum(jnp.where(lane == notes.shape[1] - 1, parts, 0.0), axis=1, keepdims=True)
    return (high * 32768.0 + low) * (-1.0 / LOG_STEP)


def moved(pairs, arrived):
    moves = [
        pltpu.make_async_copy(source, target, arrived.at[i])
        for i, (source, target) in enumerate(pairs)
    ]
    for move in moves:
        move.start()
    for move in moves:
        move.wait()


def copies_kernel(w, out, arrived):
    moved([(w, out.at[copy]) for copy in range(out.shape[0])], arrived)


def copies(w, count):
    return pl.pallas_call(
        copies_kernel,
        in_specs=[pl.BlockSpec(memory_space=pltpu.VMEM)],
        out_specs=pl.BlockSpec(memory_space=pltpu.HBM),
        out_shape=jax.ShapeDtypeStruct((count, *w.shape), w.dtype),
        scratch_shapes=[pltpu.SemaphoreType.DMA((count,))],
        compiler_params=pltpu.CompilerParams(vmem_limit_bytes=VMEM),
    )(w)


def edge_kernel(tokens, values, out, last_tokens, last_values, arrived):
    lines = pl.ds(tokens.shape[0] - ROWS, ROWS)
    moved([(tokens.at[lines, :], last_tokens), (values.at[lines, :], last_values)], arrived)
    margin, width = out.shape[0], tokens.shape[1]
    out[:, :width] = last_tokens[...].astype(jnp.float32)[ROWS - margin :, :].astype(out.dtype)
    out[:, width:] = last_values[...].astype(jnp.float32)[ROWS - margin :, :].astype(out.dtype)


def columns_of(chip, core, depth):
    return pl.ds(pl.multiple_of((2 * chip + core) * depth, 128), depth)


def project(core, hidden, tail, w, main, edge):
    depth = w.shape[1]
    for chip in range(w.shape[0]):
        some = hidden[:, chip * depth : (chip + 1) * depth]
        main += jnp.dot(some, w[chip], preferred_element_type=jnp.float32)
        some = tail[:, columns_of(chip, core, depth)]
        edge += jnp.dot(some, w[chip], preferred_element_type=jnp.float32)
    return main, edge


def partial_kernel(core, hidden, tail, w, total, rest, held, arrived):
    chips, depth, size = w.shape
    moved(
        [
            (hidden.at[:, columns_of(chip, side, depth)], to.at[:, pl.ds(chip * depth, depth)])
            for side, to in ((core[0], held), (1 - core[0], rest))
            for chip in range(chips)
        ],
        arrived,
    )
    main = jnp.zeros((hidden.shape[0], size), jnp.float32)
    edge = jnp.zeros((tail.shape[0], size), jnp.float32)
    main, edge = project(core[0], held, tail, w, main, edge)
    total[0:ROWS, :] = edge
    total[ROWS:, :] = main


def split_lanes(wide):
    high = wide.astype(jnp.bfloat16)
    low = (wide - high.astype(jnp.float32)).astype(jnp.bfloat16)
    return jnp.concatenate([high, low], axis=1)


def three_parts(wide):
    parts = []
    for _ in range(3):
        parts.append(wide.astype(jnp.bfloat16))
        wide = wide - parts[-1].astype(jnp.float32)
    return parts


def logs_of(steps):
    head_count, length = steps.shape
    earlier = lax.broadcasted_iota(jnp.int32, (length, length), 0)
    token = lax.broadcasted_iota(jnp.int32, (length, length), 1)
    upto = jnp.where(earlier <= token, 1.0, 0.0).astype(jnp.bfloat16)
    after = jnp.zeros((head_count, length), jnp.float32)
    for part in reversed(three_parts(steps)):
        after += jnp.dot(part, upto, preferred_element_type=jnp.float32)
    return after, lax.broadcasted_iota(jnp.int32, (head_count, length), 1)


def mixed_inputs(values, edge, taps, extended):
    length, channels = values.shape
    margin = taps.shape[0] - 1
    width = channels // GROUP
    extended[ROWS - margin : ROWS, :] = edge
    extended[ROWS:, :] = values[...].astype(jnp.float32)
    for part in range(GROUP):
        lanes = slice(part * width, (part + 1) * width)
        summed = jnp.zeros((length, width), jnp.float32)
        for offset in range(margin + 1):
            first = ROWS - margin + offset
            summed = (
                summed + taps[offset : offset + 1, lanes] * extended[first : first + length, lanes]
            )
        yield part, (summed * jax.nn.sigmoid(summed)).T


def weighted(mixed, weight):
    heads, length = weight.shape
    mixed = mixed.reshape(heads, mixed.shape[0] // heads, length)
    return split_lanes((mixed * weight[:, None, :]).reshape(-1, length))


def inputs_kernel(
    steps, values, before, taps, ends, end_logs, tail, extended, held, steps_held, taps_held, arrived
):
    moved([(values, held), (steps, steps_held), (taps, taps_held)], arrived)
    margin = taps.shape[0] - 1
    width = tail.shape[1]
    edge = before[...].astype(jnp.float32)
    zeros = jnp.zeros((ROWS - margin, width), jnp.float32)
    tail[...] = jnp.concatenate([zeros, edge[:, :width]], axis=0).astype(jnp.bfloat16)
    after, token = logs_of(steps_held[...])
    end_log = jnp.sum(jnp.where(token == token.shape[1] - 1, after, 0.0), axis=1, keepdims=True)
    weight = jnp.exp(end_log - after)
    end_logs[...] = jnp.broadcast_to(end_log, end_logs.shape)
    heads = weight.shape[0] // GROUP
    for part, mixed in mixed_inputs(held, edge[:, width:], taps_held, extended):
        rows = mixed.shape[0]
        some = weight[part * heads : (part + 1) * heads, :]
        ends[part * rows : (part + 1) * rows, :] = weighted(mixed, some)


def right_side(mixed_b):
    high = mixed_b.astype(jnp.bfloat16)
    low = (mixed_b - high.astype(jnp.float32)).astype(jnp.bfloat16)
    return jnp.concatenate(
        [
            jnp.concatenate([high, low], axis=1),
            jnp.concatenate([high, jnp.zeros_like(low)], axis=1),
        ],
        axis=0,
    )


def state_of(sides, right):
    both = jnp.dot(sides, right, preferred_element_type=jnp.float32)
    size = both.shape[1] // 2
    return both[:, :size] + both[:, size:]


def write_slice(sent, states, logs=None):
    heads, headdim, size = states.shape
    rows = heads * headdim // 2
    scale = scale_codes(jnp.max(jnp.abs(states), axis=1))
    sent[0:rows, :] = words_of(states * up(scale)[:, None, :]).reshape(rows, size)
    notes = scale.astype(jnp.int32)
    sent[rows:, :] = pack(notes, jnp.zeros_like(notes) if logs is None else code_logs(logs))


def read_slice(got, headdim):
    size = got.shape[1]
    half = headdim // 2
    heads = got.shape[0] // (half + 1)
    rows = heads * half
    notes = got[rows:, :]
    states = codes_of(got[0:rows, :].reshape(heads, half, size))
    return states * down(high_of(notes).astype(jnp.float32))[:, None, :], notes


def full_kernel(headdim, core, hidden, tail, w, taps, begun, ends, logs, sent, sides, extended):
    main, edge = project(1 - core[0], hidden, tail, w, begun[ROWS:, :], begun[0:ROWS, :])
    extended[0:ROWS, :] = edge
    extended[ROWS:, :] = main
    kernel = taps.shape[0]
    length, size = main.shape
    summed = jnp.zeros((length, size), jnp.float32)
    for offset in range(kernel):
        first = ROWS - kernel + 1 + offset
        summed = summed + taps[offset : offset + 1, :] * extended[first : first + length, :]
    right = right_side(summed * jax.nn.sigmoid(summed))
    sides[...] = right
    rows = ends.shape[0] // GROUP
    heads = rows // headdim
    for owner in range(GROUP):
        state = state_of(ends[owner * rows : (owner + 1) * rows, :], right)
        write_slice(
            sent.at[owner],
            state.reshape(heads, headdim, size),
            logs[owner * heads : (owner + 1) * heads, :],
        )


def kept_kernel(
    accepted, steps, values, before, taps, right, out, decay, extended, held, steps_held, taps_held, arrived
):
    moved([(values, held), (steps, steps_held), (taps, taps_held)], arrived)
    kept = accepted[0]
    after, token = logs_of(steps_held[...])
    kept_log = jnp.sum(jnp.where(token == kept - 1, after, 0.0), axis=1, keepdims=True)
    inside = token < kept
    weight = jnp.where(inside, jnp.exp(jnp.where(inside, kept_log - after, 0.0)), 0.0)
    decay[...] = jnp.broadcast_to(jnp.exp(kept_log), decay.shape)
    edge = before[...].astype(jnp.float32)[:, before.shape[1] - values.shape[1] :]
    heads = weight.shape[0] // GROUP
    for part, mixed in mixed_inputs(held, edge, taps_held, extended):
        rows = mixed.shape[0]
        some = weight[part * heads : (part + 1) * heads, :]
        out[part * rows : (part + 1) * rows, :] = state_of(weighted(mixed, some), right[...])


def group_kernel(headdim, wraps, got, prefix, decay, sent):
    goes_on = jnp.where(wraps[0] > 0, 0.0, 1.0)
    rows, size = prefix.shape[1:]
    heads = rows // headdim
    half = headdim // 2
    message = half + 1
    carried = jnp.zeros((heads, headdim, size), jnp.float32)
    passed = jnp.zeros((heads, size), jnp.float32)
    for shard in range(GROUP):
        if shard == SHIFT:
            carried = carried * goes_on
            passed = passed * goes_on
        prefix[shard] = carried.reshape(rows, size)
        decay[shard] = jnp.exp(passed) * (goes_on if shard >= SHIFT else 1.0)
        state, notes = read_slice(got.at[shard], headdim)
        log = jnp.broadcast_to(read_logs(notes), (heads, size))
        carried = jnp.exp(log)[:, None, :] * carried + state
        passed = passed + log
    scale = scale_codes(jnp.max(jnp.abs(carried), axis=1))
    words = words_of(carried * up(scale)[:, None, :])
    for head in range(heads):
        sent[head * message : head * message + half, :] = words[head]
    sent[pl.ds(half, heads, stride=message), :] = pack(scale.astype(jnp.int32), code_logs(passed))


def members_of(groups):
    rows = groups // GROUP
    return [row * GROUP + place for place in range(GROUP) for row in range(rows)]


def scan_kernel(headdim, core, got, sent, held, tops, factors, decays):
    half = headdim // 2
    message = half + 1
    groups = got.shape[0] // message
    size = got.shape[1]
    notes = got[pl.ds(half, groups, stride=message), :]
    factors[...] = down(high_of(notes).astype(jnp.float32))
    decays[...] = jnp.broadcast_to(jnp.exp(read_logs(notes)), decays.shape)
    listed = members_of(groups)
    last = listed.index(groups - 1)
    opening = codes_of(got[last * message : last * message + half, :])
    carried = opening * factors[last : last + 1, :] * jnp.where(core[0] > 0, 1.0, 0.0)
    for group in range(groups):
        slot = listed.index(group)
        held[slot * headdim : (slot + 1) * headdim, :] = carried
        tops[slot : slot + 1, :] = jnp.max(jnp.abs(carried), axis=0, keepdims=True)
        state = codes_of(got[slot * message : slot * message + half, :])
        state = state * factors[slot : slot + 1, :]
        carried = decays[slot : slot + 1, :] * carried + state
    scale = scale_codes(tops[...])
    sent[pl.ds(half, groups, stride=message), :] = lax.shift_left(scale.astype(jnp.int32), 16)
    factors[...] = up(scale)
    for group in range(groups):
        scaled = held[group * headdim : (group + 1) * headdim, :] * factors[group : group + 1, :]
        sent[group * message : group * message + half, :] = words_of(scaled)


def incoming_kernel(headdim, got, prefix, decay, sent, held, factors, staged, arrived):
    shards, rows, size = prefix.shape
    heads = rows // headdim
    half = headdim // 2
    message = half + 1
    notes = got[pl.ds(half, heads, stride=message), :]
    factors[...] = down(high_of(notes).astype(jnp.float32))
    for head in range(heads):
        state = codes_of(got[head * message : head * message + half, :])
        held[head] = state * factors[head : head + 1, :]
    for shard in range(shards):
        local = prefix[shard].reshape(heads, headdim, size)
        write_slice(staged.at[shard], decay[shard][:, None, :] * held[...] + local)
        pltpu.make_async_copy(staged.at[shard], sent.at[shard], arrived.at[shard]).start()
    for shard in range(shards):
        pltpu.make_async_copy(staged.at[shard], sent.at[shard], arrived.at[shard]).wait()


def final_kernel(headdim, got, kept, part, out, staged, arrived):
    rows = part.shape[0] // GROUP
    size = part.shape[1]
    heads = rows // headdim
    moves = []
    for owner in range(GROUP):
        state, _ = read_slice(got.at[owner], headdim)
        scaled = kept[owner * heads : (owner + 1) * heads, :][:, None, :] * state
        lines = slice(owner * rows, (owner + 1) * rows)
        staged[lines, :] = scaled.reshape(rows, size) + part[lines, :]
        lines = pl.ds(owner * rows, rows)
        moves.append(
            pltpu.make_async_copy(staged.at[lines, :], out.at[lines, :], arrived.at[owner])
        )
        moves[-1].start()
    for move in moves:
        move.wait()


def on_device(hidden, inputs, w_b, conv_x, conv_b, log_decay, accepted):
    tokens = hidden[0]
    values = inputs[0]
    length, width = tokens.shape
    channels = values.shape[1]
    margin = conv_x.shape[0] - 1
    head_count = log_decay.shape[2]
    headdim = channels // head_count
    size = w_b.shape[1]
    message = headdim // 2 + 1
    heads = head_count // GROUP
    rows = heads * headdim
    f32, bf16, i32 = jnp.float32, jnp.bfloat16, jnp.int32
    array = jax.ShapeDtypeStruct
    shards = lax.axis_size("seq")
    parts = lax.axis_size("fsdp")
    group_count = shards // GROUP

    def device(side, part, place):
        return (place + SHIFT * side) % shards * parts + 2 * part + side

    sides = [(side, part) for part in range(parts // 2) for side in range(2)]
    near = [
        [device(side, part, group * GROUP + i) for i in range(GROUP)]
        for side, part in sides
        for group in range(group_count)
    ]
    far = [
        [device(side, part, group * GROUP + i) for group in members_of(group_count)]
        for side, part in sides
        for i in range(GROUP)
    ]
    core = lax.axis_index("fsdp") % 2
    place = (lax.axis_index("seq") - SHIFT * core) % shards
    wraps = jnp.reshape(core * (place // GROUP == group_count - 1), (1,)).astype(i32)
    core = jnp.reshape(core, (1,)).astype(i32)

    def exchange(sent, members):
        return lax.all_to_all(sent, ("seq", "fsdp"), 0, 0, axis_index_groups=members)

    def exchange_heads(sent):
        return exchange(sent.reshape(heads, 1, message * size), far).reshape(sent.shape)

    chips = [[i for i in range(parts) if i % 2 == c] for c in range(2)]
    w_copies = copies(w_b, parts // 2)
    w_own = lax.all_to_all(w_copies, "fsdp", 0, 0, axis_index_groups=chips)
    dma = pltpu.SemaphoreType.DMA
    edge = call(
        edge_kernel,
        tokens,
        values,
        far=(0, 1),
        out=array((margin, width + channels), bf16),
        scratch=[pltpu.VMEM((ROWS, width), bf16), pltpu.VMEM((ROWS, channels), bf16), dma((2,))],
    )
    before = lax.ppermute(edge, "seq", [(i, i + 1) for i in range(shards - 1)])

    steps = log_decay[0].T
    wide = array((head_count, size), f32)
    scratch = [
        pltpu.VMEM((ROWS + length, channels), f32),
        pltpu.VMEM(values.shape, values.dtype),
        pltpu.VMEM(steps.shape, f32),
        pltpu.VMEM(conv_x.shape, f32),
        dma((3,)),
    ]
    ends_x, end_logs, tail = call(
        inputs_kernel,
        steps,
        values,
        before,
        conv_x,
        far=(0, 1, 3),
        out=[array((channels, 2 * length), bf16), wide, array((ROWS, width), bf16)],
        scratch=scratch,
    )

    w_own, before, core, wraps = lax.optimization_barrier((w_own, before, core, wraps))
    w_other = lax.ppermute(w_own, "fsdp", [(i, i ^ 1) for i in range(parts)])
    begun, rest = call(
        partial_kernel,
        core,
        tokens,
        tail,
        w_own,
        far=(1,),
        out=[array((ROWS + length, size), f32), array((length, width // 2), bf16)],
        scratch=[pltpu.VMEM((length, width // 2), bf16), dma((parts,))],
    )

    slices = array((GROUP, heads * message, size), i32)
    sent, right = call(
        functools.partial(full_kernel, headdim),
        core,
        rest,
        tail,
        w_other,
        conv_b,
        begun,
        ends_x,
        end_logs,
        out=[slices, array((2 * length, 2 * size), bf16)],
        scratch=[pltpu.VMEM((ROWS + length, size), f32)],
    )
    prefix, decay, sent = call(
        functools.partial(group_kernel, headdim),
        wraps,
        exchange(sent, near),
        out=[
            array((GROUP, rows, size), f32),
            array((GROUP, heads, size), f32),
            array((heads * message, size), i32),
        ],
    )
    part, kept_decay = call(
        kept_kernel,
        accepted[0],
        steps,
        values,
        before,
        conv_x,
        right,
        far=(1, 2, 4),
        out=[array((channels, size), f32), wide],
        scratch=scratch,
    )

    sent = call(
        functools.partial(scan_kernel, headdim),
        core,
        exchange_heads(sent),
        out=array(sent.shape, i32),
        scratch=[pltpu.VMEM((group_count * headdim, size), f32)]
        + [pltpu.VMEM((group_count, size), f32)] * 3,
    )
    sent = call(
        functools.partial(incoming_kernel, headdim),
        exchange_heads(sent),
        prefix,
        decay,
        out=slices,
        out_space=pltpu.HBM,
        scratch=[
            pltpu.VMEM((heads, headdim, size), f32),
            pltpu.VMEM((heads, size), f32),
            pltpu.VMEM(slices.shape, i32),
            dma((GROUP,)),
        ],
    )
    final = call(
        functools.partial(final_kernel, headdim),
        exchange(sent, near),
        kept_decay,
        part,
        out=array((channels, size), f32),
        out_space=pltpu.HBM,
        scratch=[pltpu.VMEM((channels, size), f32), dma((GROUP,))],
    )
    return final.reshape(1, 1, head_count, headdim, size)


def solution(mesh):
    placed = (
        P("fsdp", "seq", None),
        P("fsdp", "seq", None),
        P("fsdp", None),
        P(),
        P(),
        P("fsdp", "seq", None),
        P("fsdp", "seq"),
    )
    return jax.shard_map(
        on_device,
        mesh=mesh,
        in_specs=placed,
        out_specs=P("fsdp", "seq", None, None, None),
        check_vma=False,
    )
```

```python
import functools

import jax
import jax.numpy as jnp
from jax import lax
from jax.experimental import pallas as pl
from jax.experimental.pallas import tpu as pltpu
from jax.sharding import PartitionSpec as P

ROWS = 16
GROUP = 4
SHIFT = 2
TOP = 32760.0
FINE = 128.0
LOG_STEP = float(2**19)
VMEM = 12 * 1024 * 1024


def call(kernel, *args, out, scratch=(), far=(), out_space=pltpu.VMEM):
    places = [
        pltpu.SMEM if a.shape == (1,) else pltpu.HBM if i in far else pltpu.VMEM
        for i, a in enumerate(args)
    ]
    return pl.pallas_call(
        kernel,
        in_specs=[pl.BlockSpec(memory_space=place) for place in places],
        out_specs=jax.tree.map(lambda _: pl.BlockSpec(memory_space=out_space), out),
        out_shape=out,
        scratch_shapes=scratch,
        compiler_params=pltpu.CompilerParams(vmem_limit_bytes=VMEM),
    )(*args)


def scale_codes(top):
    return jnp.ceil(jnp.log2(jnp.maximum(top, 1e-33)) * FINE)


def up(scale):
    return TOP * jnp.exp2(scale * (-1.0 / FINE))


def down(scale):
    return jnp.exp2(scale * (1.0 / FINE)) * (1.0 / TOP)


def pack(high, low):
    return lax.shift_left(high, 16) | (low & 0xFFFF)


def high_of(words):
    return lax.shift_right_arithmetic(words, 16)


def low_of(words):
    return lax.shift_right_arithmetic(lax.shift_left(words, 16), 16)


def words_of(scaled):
    codes = jnp.round(scaled).astype(jnp.int32)
    half = codes.shape[-2] // 2
    return pack(codes[..., :half, :], codes[..., half:, :])


def codes_of(words):
    return jnp.concatenate([high_of(words), low_of(words)], axis=-2).astype(jnp.float32)


def code_logs(logs):
    whole = jnp.round(logs * -LOG_STEP).astype(jnp.int32)
    lane = lax.broadcasted_iota(jnp.int32, logs.shape, 1)
    high = lax.shift_right_logical(whole, 15)
    return jnp.where(lane < logs.shape[1] // 2, high, whole & 0x7FFF)


def read_logs(notes):
    lane = lax.broadcasted_iota(jnp.int32, notes.shape, 1)
    parts = (notes & 0xFFFF).astype(jnp.float32)
    high = jnp.sum(jnp.where(lane == 0, parts, 0.0), axis=1, keepdims=True)
    low = jnp.sum(jnp.where(lane == notes.shape[1] - 1, parts, 0.0), axis=1, keepdims=True)
    return (high * 32768.0 + low) * (-1.0 / LOG_STEP)


def moved(pairs, arrived):
    moves = [
        pltpu.make_async_copy(source, target, arrived.at[i])
        for i, (source, target) in enumerate(pairs)
    ]
    for move in moves:
        move.start()
    for move in moves:
        move.wait()


def copies_kernel(w, out, arrived):
    moved([(w, out.at[copy]) for copy in range(out.shape[0])], arrived)


def copies(w, count):
    return pl.pallas_call(
        copies_kernel,
        in_specs=[pl.BlockSpec(memory_space=pltpu.VMEM)],
        out_specs=pl.BlockSpec(memory_space=pltpu.HBM),
        out_shape=jax.ShapeDtypeStruct((count, *w.shape), w.dtype),
        scratch_shapes=[pltpu.SemaphoreType.DMA((count,))],
        compiler_params=pltpu.CompilerParams(vmem_limit_bytes=VMEM),
    )(w)


def edge_kernel(tokens, values, out, last_tokens, last_values, arrived):
    lines = pl.ds(tokens.shape[0] - ROWS, ROWS)
    moved([(tokens.at[lines, :], last_tokens), (values.at[lines, :], last_values)], arrived)
    margin, width = out.shape[0], tokens.shape[1]
    out[:, :width] = last_tokens[...].astype(jnp.float32)[ROWS - margin :, :].astype(out.dtype)
    out[:, width:] = last_values[...].astype(jnp.float32)[ROWS - margin :, :].astype(out.dtype)


def columns_of(chip, core, depth):
    return pl.ds(pl.multiple_of((2 * chip + core) * depth, 128), depth)


def project(core, hidden, tail, w, main, edge):
    depth = w.shape[1]
    for chip in range(w.shape[0]):
        some = hidden[:, chip * depth : (chip + 1) * depth]
        main += jnp.dot(some, w[chip], preferred_element_type=jnp.float32)
        some = tail[:, columns_of(chip, core, depth)]
        edge += jnp.dot(some, w[chip], preferred_element_type=jnp.float32)
    return main, edge


def partial_kernel(core, hidden, tail, w, total, rest, held, arrived):
    chips, depth, size = w.shape
    moved(
        [
            (hidden.at[:, columns_of(chip, side, depth)], to.at[:, pl.ds(chip * depth, depth)])
            for side, to in ((core[0], held), (1 - core[0], rest))
            for chip in range(chips)
        ],
        arrived,
    )
    main = jnp.zeros((hidden.shape[0], size), jnp.float32)
    edge = jnp.zeros((tail.shape[0], size), jnp.float32)
    main, edge = project(core[0], held, tail, w, main, edge)
    total[0:ROWS, :] = edge
    total[ROWS:, :] = main


def split_lanes(wide):
    high = wide.astype(jnp.bfloat16)
    low = (wide - high.astype(jnp.float32)).astype(jnp.bfloat16)
    return jnp.concatenate([high, low], axis=1)


def three_parts(wide):
    parts = []
    for _ in range(3):
        parts.append(wide.astype(jnp.bfloat16))
        wide = wide - parts[-1].astype(jnp.float32)
    return parts


def logs_of(steps):
    head_count, length = steps.shape
    earlier = lax.broadcasted_iota(jnp.int32, (length, length), 0)
    token = lax.broadcasted_iota(jnp.int32, (length, length), 1)
    upto = jnp.where(earlier <= token, 1.0, 0.0).astype(jnp.bfloat16)
    after = jnp.zeros((head_count, length), jnp.float32)
    for part in reversed(three_parts(steps)):
        after += jnp.dot(part, upto, preferred_element_type=jnp.float32)
    return after, lax.broadcasted_iota(jnp.int32, (head_count, length), 1)


def mixed_inputs(values, edge, taps, extended):
    length, channels = values.shape
    margin = taps.shape[0] - 1
    width = channels // GROUP
    extended[ROWS - margin : ROWS, :] = edge
    extended[ROWS:, :] = values[...].astype(jnp.float32)
    for part in range(GROUP):
        lanes = slice(part * width, (part + 1) * width)
        summed = jnp.zeros((length, width), jnp.float32)
        for offset in range(margin + 1):
            first = ROWS - margin + offset
            summed = (
                summed + taps[offset : offset + 1, lanes] * extended[first : first + length, lanes]
            )
        yield part, (summed * jax.nn.sigmoid(summed)).T


def weighted(mixed, weight):
    heads, length = weight.shape
    mixed = mixed.reshape(heads, mixed.shape[0] // heads, length)
    return split_lanes((mixed * weight[:, None, :]).reshape(-1, length))


def inputs_kernel(
    steps, values, before, taps, ends, end_logs, tail, extended, held, steps_held, taps_held, arrived
):
    moved([(values, held), (steps, steps_held), (taps, taps_held)], arrived)
    margin = taps.shape[0] - 1
    width = tail.shape[1]
    edge = before[...].astype(jnp.float32)
    zeros = jnp.zeros((ROWS - margin, width), jnp.float32)
    tail[...] = jnp.concatenate([zeros, edge[:, :width]], axis=0).astype(jnp.bfloat16)
    after, token = logs_of(steps_held[...])
    end_log = jnp.sum(jnp.where(token == token.shape[1] - 1, after, 0.0), axis=1, keepdims=True)
    weight = jnp.exp(end_log - after)
    end_logs[...] = jnp.broadcast_to(end_log, end_logs.shape)
    heads = weight.shape[0] // GROUP
    for part, mixed in mixed_inputs(held, edge[:, width:], taps_held, extended):
        rows = mixed.shape[0]
        some = weight[part * heads : (part + 1) * heads, :]
        ends[part * rows : (part + 1) * rows, :] = weighted(mixed, some)


def right_side(mixed_b):
    high = mixed_b.astype(jnp.bfloat16)
    low = (mixed_b - high.astype(jnp.float32)).astype(jnp.bfloat16)
    return jnp.concatenate(
        [
            jnp.concatenate([high, low], axis=1),
            jnp.concatenate([high, jnp.zeros_like(low)], axis=1),
        ],
        axis=0,
    )


def state_of(sides, right):
    both = jnp.dot(sides, right, preferred_element_type=jnp.float32)
    size = both.shape[1] // 2
    return both[:, :size] + both[:, size:]


def write_slice(sent, states, logs=None):
    heads, headdim, size = states.shape
    rows = heads * headdim // 2
    scale = scale_codes(jnp.max(jnp.abs(states), axis=1))
    sent[0:rows, :] = words_of(states * up(scale)[:, None, :]).reshape(rows, size)
    notes = scale.astype(jnp.int32)
    sent[rows:, :] = pack(notes, jnp.zeros_like(notes) if logs is None else code_logs(logs))


def read_slice(got, headdim):
    size = got.shape[1]
    half = headdim // 2
    heads = got.shape[0] // (half + 1)
    rows = heads * half
    notes = got[rows:, :]
    states = codes_of(got[0:rows, :].reshape(heads, half, size))
    return states * down(high_of(notes).astype(jnp.float32))[:, None, :], notes


def full_kernel(headdim, core, hidden, tail, w, taps, begun, ends, logs, sent, sides, extended):
    main, edge = project(1 - core[0], hidden, tail, w, begun[ROWS:, :], begun[0:ROWS, :])
    extended[0:ROWS, :] = edge
    extended[ROWS:, :] = main
    kernel = taps.shape[0]
    length, size = main.shape
    summed = jnp.zeros((length, size), jnp.float32)
    for offset in range(kernel):
        first = ROWS - kernel + 1 + offset
        summed = summed + taps[offset : offset + 1, :] * extended[first : first + length, :]
    right = right_side(summed * jax.nn.sigmoid(summed))
    sides[...] = right
    rows = ends.shape[0] // GROUP
    heads = rows // headdim
    for owner in range(GROUP):
        state = state_of(ends[owner * rows : (owner + 1) * rows, :], right)
        write_slice(
            sent.at[owner],
            state.reshape(heads, headdim, size),
            logs[owner * heads : (owner + 1) * heads, :],
        )


def kept_kernel(
    accepted, steps, values, before, taps, right, out, decay, extended, held, steps_held, taps_held, arrived
):
    moved([(values, held), (steps, steps_held), (taps, taps_held)], arrived)
    kept = accepted[0]
    after, token = logs_of(steps_held[...])
    kept_log = jnp.sum(jnp.where(token == kept - 1, after, 0.0), axis=1, keepdims=True)
    inside = token < kept
    weight = jnp.where(inside, jnp.exp(jnp.where(inside, kept_log - after, 0.0)), 0.0)
    decay[...] = jnp.broadcast_to(jnp.exp(kept_log), decay.shape)
    edge = before[...].astype(jnp.float32)[:, before.shape[1] - values.shape[1] :]
    heads = weight.shape[0] // GROUP
    for part, mixed in mixed_inputs(held, edge, taps_held, extended):
        rows = mixed.shape[0]
        some = weight[part * heads : (part + 1) * heads, :]
        out[part * rows : (part + 1) * rows, :] = state_of(weighted(mixed, some), right[...])


def group_kernel(headdim, wraps, got, prefix, decay, sent):
    goes_on = jnp.where(wraps[0] > 0, 0.0, 1.0)
    rows, size = prefix.shape[1:]
    heads = rows // headdim
    half = headdim // 2
    message = half + 1
    carried = jnp.zeros((heads, headdim, size), jnp.float32)
    passed = jnp.zeros((heads, size), jnp.float32)
    for shard in range(GROUP):
        if shard == SHIFT:
            carried = carried * goes_on
            passed = passed * goes_on
        prefix[shard] = carried.reshape(rows, size)
        decay[shard] = jnp.exp(passed) * (goes_on if shard >= SHIFT else 1.0)
        state, notes = read_slice(got.at[shard], headdim)
        log = jnp.broadcast_to(read_logs(notes), (heads, size))
        carried = jnp.exp(log)[:, None, :] * carried + state
        passed = passed + log
    scale = scale_codes(jnp.max(jnp.abs(carried), axis=1))
    words = words_of(carried * up(scale)[:, None, :])
    for head in range(heads):
        sent[head * message : head * message + half, :] = words[head]
    sent[pl.ds(half, heads, stride=message), :] = pack(scale.astype(jnp.int32), code_logs(passed))


def members_of(groups):
    rows = groups // GROUP
    places = [(place + GROUP // 2) % GROUP for place in range(GROUP)]
    return [row * GROUP + place for place in places for row in reversed(range(rows))]


def scan_kernel(headdim, core, got, sent, held, tops, factors, decays):
    half = headdim // 2
    message = half + 1
    groups = got.shape[0] // message
    size = got.shape[1]
    notes = got[pl.ds(half, groups, stride=message), :]
    factors[...] = down(high_of(notes).astype(jnp.float32))
    decays[...] = jnp.broadcast_to(jnp.exp(read_logs(notes)), decays.shape)
    listed = members_of(groups)
    last = listed.index(groups - 1)
    opening = codes_of(got[last * message : last * message + half, :])
    carried = opening * factors[last : last + 1, :] * jnp.where(core[0] > 0, 1.0, 0.0)
    for group in range(groups):
        slot = listed.index(group)
        held[slot * headdim : (slot + 1) * headdim, :] = carried
        tops[slot : slot + 1, :] = jnp.max(jnp.abs(carried), axis=0, keepdims=True)
        state = codes_of(got[slot * message : slot * message + half, :])
        state = state * factors[slot : slot + 1, :]
        carried = decays[slot : slot + 1, :] * carried + state
    scale = scale_codes(tops[...])
    sent[pl.ds(half, groups, stride=message), :] = lax.shift_left(scale.astype(jnp.int32), 16)
    factors[...] = up(scale)
    for group in range(groups):
        scaled = held[group * headdim : (group + 1) * headdim, :] * factors[group : group + 1, :]
        sent[group * message : group * message + half, :] = words_of(scaled)


def incoming_kernel(headdim, got, prefix, decay, sent, held, factors, staged, arrived):
    shards, rows, size = prefix.shape
    heads = rows // headdim
    half = headdim // 2
    message = half + 1
    notes = got[pl.ds(half, heads, stride=message), :]
    factors[...] = down(high_of(notes).astype(jnp.float32))
    for head in range(heads):
        state = codes_of(got[head * message : head * message + half, :])
        held[head] = state * factors[head : head + 1, :]
    for shard in range(shards):
        local = prefix[shard].reshape(heads, headdim, size)
        write_slice(staged.at[shard], decay[shard][:, None, :] * held[...] + local)
        pltpu.make_async_copy(staged.at[shard], sent.at[shard], arrived.at[shard]).start()
    for shard in range(shards):
        pltpu.make_async_copy(staged.at[shard], sent.at[shard], arrived.at[shard]).wait()


def final_kernel(headdim, got, kept, part, out, staged, arrived):
    rows = part.shape[0] // GROUP
    size = part.shape[1]
    heads = rows // headdim
    moves = []
    for owner in range(GROUP):
        state, _ = read_slice(got.at[owner], headdim)
        scaled = kept[owner * heads : (owner + 1) * heads, :][:, None, :] * state
        lines = slice(owner * rows, (owner + 1) * rows)
        staged[lines, :] = scaled.reshape(rows, size) + part[lines, :]
        lines = pl.ds(owner * rows, rows)
        moves.append(
            pltpu.make_async_copy(staged.at[lines, :], out.at[lines, :], arrived.at[owner])
        )
        moves[-1].start()
    for move in moves:
        move.wait()


def on_device(hidden, inputs, w_b, conv_x, conv_b, log_decay, accepted):
    tokens = hidden[0]
    values = inputs[0]
    length, width = tokens.shape
    channels = values.shape[1]
    margin = conv_x.shape[0] - 1
    head_count = log_decay.shape[2]
    headdim = channels // head_count
    size = w_b.shape[1]
    message = headdim // 2 + 1
    heads = head_count // GROUP
    rows = heads * headdim
    f32, bf16, i32 = jnp.float32, jnp.bfloat16, jnp.int32
    array = jax.ShapeDtypeStruct
    shards = lax.axis_size("seq")
    parts = lax.axis_size("fsdp")
    group_count = shards // GROUP

    def device(side, part, place):
        return (place + SHIFT * side) % shards * parts + 2 * part + side

    sides = [(side, part) for part in range(parts // 2) for side in range(2)]
    near = [
        [device(side, part, group * GROUP + i) for i in range(GROUP)]
        for side, part in sides
        for group in range(group_count)
    ]
    far = [
        [device(side, part, group * GROUP + i) for group in members_of(group_count)]
        for side, part in sides
        for i in range(GROUP)
    ]
    core = lax.axis_index("fsdp") % 2
    place = (lax.axis_index("seq") - SHIFT * core) % shards
    wraps = jnp.reshape(core * (place // GROUP == group_count - 1), (1,)).astype(i32)
    core = jnp.reshape(core, (1,)).astype(i32)

    def exchange(sent, members):
        return lax.all_to_all(sent, ("seq", "fsdp"), 0, 0, axis_index_groups=members)

    def exchange_heads(sent):
        return exchange(sent.reshape(heads, 1, message * size), far).reshape(sent.shape)

    chips = [[i for i in range(parts) if i % 2 == c] for c in range(2)]
    w_copies = copies(w_b, parts // 2)
    w_own = lax.all_to_all(w_copies, "fsdp", 0, 0, axis_index_groups=chips)
    dma = pltpu.SemaphoreType.DMA
    edge = call(
        edge_kernel,
        tokens,
        values,
        far=(0, 1),
        out=array((margin, width + channels), bf16),
        scratch=[pltpu.VMEM((ROWS, width), bf16), pltpu.VMEM((ROWS, channels), bf16), dma((2,))],
    )
    before = lax.ppermute(edge, "seq", [(i, i + 1) for i in range(shards - 1)])

    steps = log_decay[0].T
    wide = array((head_count, size), f32)
    scratch = [
        pltpu.VMEM((ROWS + length, channels), f32),
        pltpu.VMEM(values.shape, values.dtype),
        pltpu.VMEM(steps.shape, f32),
        pltpu.VMEM(conv_x.shape, f32),
        dma((3,)),
    ]
    ends_x, end_logs, tail = call(
        inputs_kernel,
        steps,
        values,
        before,
        conv_x,
        far=(0, 1, 3),
        out=[array((channels, 2 * length), bf16), wide, array((ROWS, width), bf16)],
        scratch=scratch,
    )

    w_own, before, core, wraps = lax.optimization_barrier((w_own, before, core, wraps))
    w_other = lax.ppermute(w_own, "fsdp", [(i, i ^ 1) for i in range(parts)])
    begun, rest = call(
        partial_kernel,
        core,
        tokens,
        tail,
        w_own,
        far=(1,),
        out=[array((ROWS + length, size), f32), array((length, width // 2), bf16)],
        scratch=[pltpu.VMEM((length, width // 2), bf16), dma((parts,))],
    )

    slices = array((GROUP, heads * message, size), i32)
    sent, right = call(
        functools.partial(full_kernel, headdim),
        core,
        rest,
        tail,
        w_other,
        conv_b,
        begun,
        ends_x,
        end_logs,
        out=[slices, array((2 * length, 2 * size), bf16)],
        scratch=[pltpu.VMEM((ROWS + length, size), f32)],
    )
    prefix, decay, sent = call(
        functools.partial(group_kernel, headdim),
        wraps,
        exchange(sent, near),
        out=[
            array((GROUP, rows, size), f32),
            array((GROUP, heads, size), f32),
            array((heads * message, size), i32),
        ],
    )
    part, kept_decay = call(
        kept_kernel,
        accepted[0],
        steps,
        values,
        before,
        conv_x,
        right,
        far=(1, 2, 4),
        out=[array((channels, size), f32), wide],
        scratch=scratch,
    )

    sent = call(
        functools.partial(scan_kernel, headdim),
        core,
        exchange_heads(sent),
        out=array(sent.shape, i32),
        scratch=[pltpu.VMEM((group_count * headdim, size), f32)]
        + [pltpu.VMEM((group_count, size), f32)] * 3,
    )
    sent = call(
        functools.partial(incoming_kernel, headdim),
        exchange_heads(sent),
        prefix,
        decay,
        out=slices,
        out_space=pltpu.HBM,
        scratch=[
            pltpu.VMEM((heads, headdim, size), f32),
            pltpu.VMEM((heads, size), f32),
            pltpu.VMEM(slices.shape, i32),
            dma((GROUP,)),
        ],
    )
    final = call(
        functools.partial(final_kernel, headdim),
        exchange(sent, near),
        kept_decay,
        part,
        out=array((channels, size), f32),
        out_space=pltpu.HBM,
        scratch=[pltpu.VMEM((channels, size), f32), dma((GROUP,))],
    )
    return final.reshape(1, 1, head_count, headdim, size)


def solution(mesh):
    placed = (
        P("fsdp", "seq", None),
        P("fsdp", "seq", None),
        P("fsdp", None),
        P(),
        P(),
        P("fsdp", "seq", None),
        P("fsdp", "seq"),
    )
    return jax.shard_map(
        on_device,
        mesh=mesh,
        in_specs=placed,
        out_specs=P("fsdp", "seq", None, None, None),
        check_vma=False,
    )
```

```python
import functools

import jax
import jax.numpy as jnp
from jax import lax
from jax.experimental import pallas as pl
from jax.experimental.pallas import tpu as pltpu
from jax.sharding import PartitionSpec as P

ROWS = 16
GROUP = 4
SHIFT = 2
TOP = 32760.0
FINE = 128.0
LOG_STEP = float(2**19)
VMEM = 12 * 1024 * 1024


def call(kernel, *args, out, scratch=(), far=(), out_space=pltpu.VMEM):
    places = [
        pltpu.SMEM if a.shape == (1,) else pltpu.HBM if i in far else pltpu.VMEM
        for i, a in enumerate(args)
    ]
    return pl.pallas_call(
        kernel,
        in_specs=[pl.BlockSpec(memory_space=place) for place in places],
        out_specs=jax.tree.map(lambda _: pl.BlockSpec(memory_space=out_space), out),
        out_shape=out,
        scratch_shapes=scratch,
        compiler_params=pltpu.CompilerParams(vmem_limit_bytes=VMEM),
    )(*args)


def scale_codes(top):
    return jnp.ceil(jnp.log2(jnp.maximum(top, 1e-33)) * FINE)


def up(scale):
    return TOP * jnp.exp2(scale * (-1.0 / FINE))


def down(scale):
    return jnp.exp2(scale * (1.0 / FINE)) * (1.0 / TOP)


def pack(high, low):
    return lax.shift_left(high, 16) | (low & 0xFFFF)


def high_of(words):
    return lax.shift_right_arithmetic(words, 16)


def low_of(words):
    return lax.shift_right_arithmetic(lax.shift_left(words, 16), 16)


def words_of(scaled):
    codes = jnp.round(scaled).astype(jnp.int32)
    half = codes.shape[-2] // 2
    return pack(codes[..., :half, :], codes[..., half:, :])


def codes_of(words):
    return jnp.concatenate([high_of(words), low_of(words)], axis=-2).astype(jnp.float32)


def code_logs(logs):
    whole = jnp.round(logs * -LOG_STEP).astype(jnp.int32)
    lane = lax.broadcasted_iota(jnp.int32, logs.shape, 1)
    high = lax.shift_right_logical(whole, 15)
    return jnp.where(lane < logs.shape[1] // 2, high, whole & 0x7FFF)


def read_logs(notes):
    lane = lax.broadcasted_iota(jnp.int32, notes.shape, 1)
    parts = (notes & 0xFFFF).astype(jnp.float32)
    high = jnp.sum(jnp.where(lane == 0, parts, 0.0), axis=1, keepdims=True)
    low = jnp.sum(jnp.where(lane == notes.shape[1] - 1, parts, 0.0), axis=1, keepdims=True)
    return (high * 32768.0 + low) * (-1.0 / LOG_STEP)


def moved(pairs, arrived):
    moves = [
        pltpu.make_async_copy(source, target, arrived.at[i])
        for i, (source, target) in enumerate(pairs)
    ]
    for move in moves:
        move.start()
    for move in moves:
        move.wait()


def copies_kernel(w, out, arrived):
    moved([(w, out.at[copy]) for copy in range(out.shape[0])], arrived)


def copies(w, count):
    return pl.pallas_call(
        copies_kernel,
        in_specs=[pl.BlockSpec(memory_space=pltpu.VMEM)],
        out_specs=pl.BlockSpec(memory_space=pltpu.HBM),
        out_shape=jax.ShapeDtypeStruct((count, *w.shape), w.dtype),
        scratch_shapes=[pltpu.SemaphoreType.DMA((count,))],
        compiler_params=pltpu.CompilerParams(vmem_limit_bytes=VMEM),
    )(w)


def edge_kernel(tokens, values, out, last_tokens, last_values, arrived):
    lines = pl.ds(tokens.shape[0] - ROWS, ROWS)
    moved([(tokens.at[lines, :], last_tokens), (values.at[lines, :], last_values)], arrived)
    margin, width = out.shape[0], tokens.shape[1]
    out[:, :width] = last_tokens[...].astype(jnp.float32)[ROWS - margin :, :].astype(out.dtype)
    out[:, width:] = last_values[...].astype(jnp.float32)[ROWS - margin :, :].astype(out.dtype)


def columns_of(chip, core, depth):
    return pl.ds(pl.multiple_of((2 * chip + core) * depth, 128), depth)


def project(core, hidden, tail, w, main, edge):
    depth = w.shape[1]
    for chip in range(w.shape[0]):
        some = hidden[:, chip * depth : (chip + 1) * depth]
        main += jnp.dot(some, w[chip], preferred_element_type=jnp.float32)
        some = tail[:, columns_of(chip, core, depth)]
        edge += jnp.dot(some, w[chip], preferred_element_type=jnp.float32)
    return main, edge


def partial_kernel(core, hidden, tail, w, total, rest, held, arrived):
    chips, depth, size = w.shape
    moved(
        [
            (hidden.at[:, columns_of(chip, side, depth)], to.at[:, pl.ds(chip * depth, depth)])
            for side, to in ((core[0], held), (1 - core[0], rest))
            for chip in range(chips)
        ],
        arrived,
    )
    main = jnp.zeros((hidden.shape[0], size), jnp.float32)
    edge = jnp.zeros((tail.shape[0], size), jnp.float32)
    main, edge = project(core[0], held, tail, w, main, edge)
    total[0:ROWS, :] = edge
    total[ROWS:, :] = main


def split_lanes(wide):
    high = wide.astype(jnp.bfloat16)
    low = (wide - high.astype(jnp.float32)).astype(jnp.bfloat16)
    return jnp.concatenate([high, low], axis=1)


def three_parts(wide):
    parts = []
    for _ in range(3):
        parts.append(wide.astype(jnp.bfloat16))
        wide = wide - parts[-1].astype(jnp.float32)
    return parts


def logs_of(steps):
    head_count, length = steps.shape
    earlier = lax.broadcasted_iota(jnp.int32, (length, length), 0)
    token = lax.broadcasted_iota(jnp.int32, (length, length), 1)
    upto = jnp.where(earlier <= token, 1.0, 0.0).astype(jnp.bfloat16)
    after = jnp.zeros((head_count, length), jnp.float32)
    for part in reversed(three_parts(steps)):
        after += jnp.dot(part, upto, preferred_element_type=jnp.float32)
    return after, lax.broadcasted_iota(jnp.int32, (head_count, length), 1)


def mixed_inputs(values, edge, taps, extended):
    length, channels = values.shape
    margin = taps.shape[0] - 1
    width = channels // GROUP
    extended[ROWS - margin : ROWS, :] = edge
    extended[ROWS:, :] = values[...].astype(jnp.float32)
    for part in range(GROUP):
        lanes = slice(part * width, (part + 1) * width)
        summed = jnp.zeros((length, width), jnp.float32)
        for offset in range(margin + 1):
            first = ROWS - margin + offset
            summed = (
                summed + taps[offset : offset + 1, lanes] * extended[first : first + length, lanes]
            )
        yield part, (summed * jax.nn.sigmoid(summed)).T


def weighted(mixed, weight):
    heads, length = weight.shape
    mixed = mixed.reshape(heads, mixed.shape[0] // heads, length)
    return split_lanes((mixed * weight[:, None, :]).reshape(-1, length))


def inputs_kernel(
    steps, values, before, taps, ends, end_logs, tail, extended, held, steps_held, taps_held, arrived
):
    moved([(values, held), (steps, steps_held), (taps, taps_held)], arrived)
    margin = taps.shape[0] - 1
    width = tail.shape[1]
    edge = before[...].astype(jnp.float32)
    zeros = jnp.zeros((ROWS - margin, width), jnp.float32)
    tail[...] = jnp.concatenate([zeros, edge[:, :width]], axis=0).astype(jnp.bfloat16)
    after, token = logs_of(steps_held[...])
    end_log = jnp.sum(jnp.where(token == token.shape[1] - 1, after, 0.0), axis=1, keepdims=True)
    weight = jnp.exp(end_log - after)
    end_logs[...] = jnp.broadcast_to(end_log, end_logs.shape)
    heads = weight.shape[0] // GROUP
    for part, mixed in mixed_inputs(held, edge[:, width:], taps_held, extended):
        rows = mixed.shape[0]
        some = weight[part * heads : (part + 1) * heads, :]
        ends[part * rows : (part + 1) * rows, :] = weighted(mixed, some)


def right_side(mixed_b):
    high = mixed_b.astype(jnp.bfloat16)
    low = (mixed_b - high.astype(jnp.float32)).astype(jnp.bfloat16)
    return jnp.concatenate(
        [
            jnp.concatenate([high, low], axis=1),
            jnp.concatenate([high, jnp.zeros_like(low)], axis=1),
        ],
        axis=0,
    )


def state_of(sides, right):
    both = jnp.dot(sides, right, preferred_element_type=jnp.float32)
    size = both.shape[1] // 2
    return both[:, :size] + both[:, size:]


def write_slice(sent, states, logs=None):
    heads, headdim, size = states.shape
    rows = heads * headdim // 2
    scale = scale_codes(jnp.max(jnp.abs(states), axis=1))
    sent[0:rows, :] = words_of(states * up(scale)[:, None, :]).reshape(rows, size)
    notes = scale.astype(jnp.int32)
    sent[rows:, :] = pack(notes, jnp.zeros_like(notes) if logs is None else code_logs(logs))


def read_slice(got, headdim):
    size = got.shape[1]
    half = headdim // 2
    heads = got.shape[0] // (half + 1)
    rows = heads * half
    notes = got[rows:, :]
    states = codes_of(got[0:rows, :].reshape(heads, half, size))
    return states * down(high_of(notes).astype(jnp.float32))[:, None, :], notes


def full_kernel(headdim, core, hidden, tail, w, taps, begun, ends, logs, sent, sides, extended):
    main, edge = project(1 - core[0], hidden, tail, w, begun[ROWS:, :], begun[0:ROWS, :])
    extended[0:ROWS, :] = edge
    extended[ROWS:, :] = main
    kernel = taps.shape[0]
    length, size = main.shape
    summed = jnp.zeros((length, size), jnp.float32)
    for offset in range(kernel):
        first = ROWS - kernel + 1 + offset
        summed = summed + taps[offset : offset + 1, :] * extended[first : first + length, :]
    right = right_side(summed * jax.nn.sigmoid(summed))
    sides[...] = right
    rows = ends.shape[0] // GROUP
    heads = rows // headdim
    for owner in range(GROUP):
        state = state_of(ends[owner * rows : (owner + 1) * rows, :], right)
        write_slice(
            sent.at[owner],
            state.reshape(heads, headdim, size),
            logs[owner * heads : (owner + 1) * heads, :],
        )


def kept_kernel(
    accepted, steps, values, before, taps, right, out, decay, extended, held, steps_held, taps_held, arrived
):
    moved([(values, held), (steps, steps_held), (taps, taps_held)], arrived)
    kept = accepted[0]
    after, token = logs_of(steps_held[...])
    kept_log = jnp.sum(jnp.where(token == kept - 1, after, 0.0), axis=1, keepdims=True)
    inside = token < kept
    weight = jnp.where(inside, jnp.exp(jnp.where(inside, kept_log - after, 0.0)), 0.0)
    decay[...] = jnp.broadcast_to(jnp.exp(kept_log), decay.shape)
    edge = before[...].astype(jnp.float32)[:, before.shape[1] - values.shape[1] :]
    heads = weight.shape[0] // GROUP
    for part, mixed in mixed_inputs(held, edge, taps_held, extended):
        rows = mixed.shape[0]
        some = weight[part * heads : (part + 1) * heads, :]
        out[part * rows : (part + 1) * rows, :] = state_of(weighted(mixed, some), right[...])


def group_kernel(headdim, wraps, got, prefix, decay, sent):
    goes_on = jnp.where(wraps[0] > 0, 0.0, 1.0)
    rows, size = prefix.shape[1:]
    heads = rows // headdim
    half = headdim // 2
    message = half + 1
    carried = jnp.zeros((heads, headdim, size), jnp.float32)
    passed = jnp.zeros((heads, size), jnp.float32)
    for shard in range(GROUP):
        if shard == SHIFT:
            carried = carried * goes_on
            passed = passed * goes_on
        prefix[shard] = carried.reshape(rows, size)
        decay[shard] = jnp.exp(passed) * (goes_on if shard >= SHIFT else 1.0)
        state, notes = read_slice(got.at[shard], headdim)
        log = jnp.broadcast_to(read_logs(notes), (heads, size))
        carried = jnp.exp(log)[:, None, :] * carried + state
        passed = passed + log
    scale = scale_codes(jnp.max(jnp.abs(carried), axis=1))
    words = words_of(carried * up(scale)[:, None, :])
    for head in range(heads):
        sent[head * message + 1 : (head + 1) * message, :] = words[head]
    sent[pl.ds(0, heads, stride=message), :] = pack(scale.astype(jnp.int32), code_logs(passed))


def members_of(groups):
    rows = groups // GROUP
    places = [(place + GROUP // 2) % GROUP for place in range(GROUP)]
    return [row * GROUP + place for place in places for row in reversed(range(rows))]


def scan_kernel(headdim, core, got, sent, held, tops, factors, decays):
    half = headdim // 2
    message = half + 1
    groups = got.shape[0] // message
    size = got.shape[1]
    notes = got[pl.ds(0, groups, stride=message), :]
    factors[...] = down(high_of(notes).astype(jnp.float32))
    decays[...] = jnp.broadcast_to(jnp.exp(read_logs(notes)), decays.shape)
    listed = members_of(groups)
    last = listed.index(groups - 1)
    opening = codes_of(got[last * message + 1 : (last + 1) * message, :])
    carried = opening * factors[last : last + 1, :] * jnp.where(core[0] > 0, 1.0, 0.0)
    for group in range(groups):
        slot = listed.index(group)
        held[slot * headdim : (slot + 1) * headdim, :] = carried
        tops[slot : slot + 1, :] = jnp.max(jnp.abs(carried), axis=0, keepdims=True)
        state = codes_of(got[slot * message + 1 : (slot + 1) * message, :])
        state = state * factors[slot : slot + 1, :]
        carried = decays[slot : slot + 1, :] * carried + state
    scale = scale_codes(tops[...])
    sent[pl.ds(0, groups, stride=message), :] = lax.shift_left(scale.astype(jnp.int32), 16)
    factors[...] = up(scale)
    for group in range(groups):
        scaled = held[group * headdim : (group + 1) * headdim, :] * factors[group : group + 1, :]
        sent[group * message + 1 : (group + 1) * message, :] = words_of(scaled)


def incoming_kernel(headdim, got, prefix, decay, sent, held, factors, staged, arrived):
    shards, rows, size = prefix.shape
    heads = rows // headdim
    half = headdim // 2
    message = half + 1
    notes = got[pl.ds(0, heads, stride=message), :]
    factors[...] = down(high_of(notes).astype(jnp.float32))
    for head in range(heads):
        state = codes_of(got[head * message + 1 : (head + 1) * message, :])
        held[head] = state * factors[head : head + 1, :]
    for shard in range(shards):
        local = prefix[shard].reshape(heads, headdim, size)
        write_slice(staged.at[shard], decay[shard][:, None, :] * held[...] + local)
        pltpu.make_async_copy(staged.at[shard], sent.at[shard], arrived.at[shard]).start()
    for shard in range(shards):
        pltpu.make_async_copy(staged.at[shard], sent.at[shard], arrived.at[shard]).wait()


def final_kernel(headdim, got, kept, part, out, staged, arrived):
    rows = part.shape[0] // GROUP
    size = part.shape[1]
    heads = rows // headdim
    moves = []
    for owner in range(GROUP):
        state, _ = read_slice(got.at[owner], headdim)
        scaled = kept[owner * heads : (owner + 1) * heads, :][:, None, :] * state
        lines = slice(owner * rows, (owner + 1) * rows)
        staged[lines, :] = scaled.reshape(rows, size) + part[lines, :]
        lines = pl.ds(owner * rows, rows)
        moves.append(
            pltpu.make_async_copy(staged.at[lines, :], out.at[lines, :], arrived.at[owner])
        )
        moves[-1].start()
    for move in moves:
        move.wait()


def on_device(hidden, inputs, w_b, conv_x, conv_b, log_decay, accepted):
    tokens = hidden[0]
    values = inputs[0]
    length, width = tokens.shape
    channels = values.shape[1]
    margin = conv_x.shape[0] - 1
    head_count = log_decay.shape[2]
    headdim = channels // head_count
    size = w_b.shape[1]
    message = headdim // 2 + 1
    heads = head_count // GROUP
    rows = heads * headdim
    f32, bf16, i32 = jnp.float32, jnp.bfloat16, jnp.int32
    array = jax.ShapeDtypeStruct
    shards = lax.axis_size("seq")
    parts = lax.axis_size("fsdp")
    group_count = shards // GROUP

    def device(side, part, place):
        return (place + SHIFT * side) % shards * parts + 2 * part + side

    sides = [(side, part) for part in range(parts // 2) for side in range(2)]
    near = [
        [device(side, part, group * GROUP + i) for i in range(GROUP)]
        for side, part in sides
        for group in range(group_count)
    ]
    far = [
        [device(side, part, group * GROUP + i) for group in members_of(group_count)]
        for side, part in sides
        for i in range(GROUP)
    ]
    core = lax.axis_index("fsdp") % 2
    place = (lax.axis_index("seq") - SHIFT * core) % shards
    wraps = jnp.reshape(core * (place // GROUP == group_count - 1), (1,)).astype(i32)
    core = jnp.reshape(core, (1,)).astype(i32)

    def exchange(sent, members):
        return lax.all_to_all(sent, ("seq", "fsdp"), 0, 0, axis_index_groups=members)

    def exchange_heads(sent):
        return exchange(sent.reshape(heads, 1, message * size), far).reshape(sent.shape)

    chips = [[i for i in range(parts) if i % 2 == c] for c in range(2)]
    w_copies = copies(w_b, parts // 2)
    w_own = lax.all_to_all(w_copies, "fsdp", 0, 0, axis_index_groups=chips)
    dma = pltpu.SemaphoreType.DMA
    edge = call(
        edge_kernel,
        tokens,
        values,
        far=(0, 1),
        out=array((margin, width + channels), bf16),
        scratch=[pltpu.VMEM((ROWS, width), bf16), pltpu.VMEM((ROWS, channels), bf16), dma((2,))],
    )
    before = lax.ppermute(edge, "seq", [(i, i + 1) for i in range(shards - 1)])

    steps = log_decay[0].T
    wide = array((head_count, size), f32)
    scratch = [
        pltpu.VMEM((ROWS + length, channels), f32),
        pltpu.VMEM(values.shape, values.dtype),
        pltpu.VMEM(steps.shape, f32),
        pltpu.VMEM(conv_x.shape, f32),
        dma((3,)),
    ]
    ends_x, end_logs, tail = call(
        inputs_kernel,
        steps,
        values,
        before,
        conv_x,
        far=(0, 1, 3),
        out=[array((channels, 2 * length), bf16), wide, array((ROWS, width), bf16)],
        scratch=scratch,
    )

    w_own, before, core, wraps = lax.optimization_barrier((w_own, before, core, wraps))
    w_other = lax.ppermute(w_own, "fsdp", [(i, i ^ 1) for i in range(parts)])
    begun, rest = call(
        partial_kernel,
        core,
        tokens,
        tail,
        w_own,
        far=(1,),
        out=[array((ROWS + length, size), f32), array((length, width // 2), bf16)],
        scratch=[pltpu.VMEM((length, width // 2), bf16), dma((parts,))],
    )

    slices = array((GROUP, heads * message, size), i32)
    sent, right = call(
        functools.partial(full_kernel, headdim),
        core,
        rest,
        tail,
        w_other,
        conv_b,
        begun,
        ends_x,
        end_logs,
        out=[slices, array((2 * length, 2 * size), bf16)],
        scratch=[pltpu.VMEM((ROWS + length, size), f32)],
    )
    prefix, decay, sent = call(
        functools.partial(group_kernel, headdim),
        wraps,
        exchange(sent, near),
        out=[
            array((GROUP, rows, size), f32),
            array((GROUP, heads, size), f32),
            array((heads * message, size), i32),
        ],
    )
    part, kept_decay = call(
        kept_kernel,
        accepted[0],
        steps,
        values,
        before,
        conv_x,
        right,
        far=(1, 2, 4),
        out=[array((channels, size), f32), wide],
        scratch=scratch,
    )

    sent = call(
        functools.partial(scan_kernel, headdim),
        core,
        exchange_heads(sent),
        out=array(sent.shape, i32),
        scratch=[pltpu.VMEM((group_count * headdim, size), f32)]
        + [pltpu.VMEM((group_count, size), f32)] * 3,
    )
    sent = call(
        functools.partial(incoming_kernel, headdim),
        exchange_heads(sent),
        prefix,
        decay,
        out=slices,
        out_space=pltpu.HBM,
        scratch=[
            pltpu.VMEM((heads, headdim, size), f32),
            pltpu.VMEM((heads, size), f32),
            pltpu.VMEM(slices.shape, i32),
            dma((GROUP,)),
        ],
    )
    final = call(
        functools.partial(final_kernel, headdim),
        exchange(sent, near),
        kept_decay,
        part,
        out=array((channels, size), f32),
        out_space=pltpu.HBM,
        scratch=[pltpu.VMEM((channels, size), f32), dma((GROUP,))],
    )
    return final.reshape(1, 1, head_count, headdim, size)


def solution(mesh):
    placed = (
        P("fsdp", "seq", None),
        P("fsdp", "seq", None),
        P("fsdp", None),
        P(),
        P(),
        P("fsdp", "seq", None),
        P("fsdp", "seq"),
    )
    return jax.shard_map(
        on_device,
        mesh=mesh,
        in_specs=placed,
        out_specs=P("fsdp", "seq", None, None, None),
        check_vma=False,
    )
```

```python
import functools

import jax
import jax.numpy as jnp
from jax import lax
from jax.experimental import pallas as pl
from jax.experimental.pallas import tpu as pltpu
from jax.sharding import PartitionSpec as P

ROWS = 16
GROUP = 4
SHIFT = 2
TOP = 32760.0
FINE = 128.0
LOG_STEP = float(2**19)
VMEM = 12 * 1024 * 1024


def call(kernel, *args, out, scratch=(), far=(), out_space=pltpu.VMEM):
    places = [
        pltpu.SMEM if a.shape == (1,) else pltpu.HBM if i in far else pltpu.VMEM
        for i, a in enumerate(args)
    ]
    return pl.pallas_call(
        kernel,
        in_specs=[pl.BlockSpec(memory_space=place) for place in places],
        out_specs=jax.tree.map(lambda _: pl.BlockSpec(memory_space=out_space), out),
        out_shape=out,
        scratch_shapes=scratch,
        compiler_params=pltpu.CompilerParams(vmem_limit_bytes=VMEM),
    )(*args)


def scale_codes(top):
    return jnp.ceil(jnp.log2(jnp.maximum(top, 1e-33)) * FINE)


def up(scale):
    return TOP * jnp.exp2(scale * (-1.0 / FINE))


def down(scale):
    return jnp.exp2(scale * (1.0 / FINE)) * (1.0 / TOP)


def pack(high, low):
    return lax.shift_left(high, 16) | (low & 0xFFFF)


def high_of(words):
    return lax.shift_right_arithmetic(words, 16)


def low_of(words):
    return lax.shift_right_arithmetic(lax.shift_left(words, 16), 16)


def words_of(scaled):
    codes = jnp.round(scaled).astype(jnp.int32)
    half = codes.shape[-2] // 2
    return pack(codes[..., :half, :], codes[..., half:, :])


def codes_of(words):
    return jnp.concatenate([high_of(words), low_of(words)], axis=-2).astype(jnp.float32)


def code_logs(logs):
    whole = jnp.round(logs * -LOG_STEP).astype(jnp.int32)
    lane = lax.broadcasted_iota(jnp.int32, logs.shape, 1)
    high = lax.shift_right_logical(whole, 15)
    return jnp.where(lane < logs.shape[1] // 2, high, whole & 0x7FFF)


def read_logs(notes):
    lane = lax.broadcasted_iota(jnp.int32, notes.shape, 1)
    parts = (notes & 0xFFFF).astype(jnp.float32)
    high = jnp.sum(jnp.where(lane == 0, parts, 0.0), axis=1, keepdims=True)
    low = jnp.sum(jnp.where(lane == notes.shape[1] - 1, parts, 0.0), axis=1, keepdims=True)
    return (high * 32768.0 + low) * (-1.0 / LOG_STEP)


def moved(pairs, arrived):
    moves = [
        pltpu.make_async_copy(source, target, arrived.at[i])
        for i, (source, target) in enumerate(pairs)
    ]
    for move in moves:
        move.start()
    for move in moves:
        move.wait()


def copies_kernel(w, out, arrived):
    moved([(w, out.at[copy]) for copy in range(out.shape[0])], arrived)


def copies(w, count):
    return pl.pallas_call(
        copies_kernel,
        in_specs=[pl.BlockSpec(memory_space=pltpu.VMEM)],
        out_specs=pl.BlockSpec(memory_space=pltpu.HBM),
        out_shape=jax.ShapeDtypeStruct((count, *w.shape), w.dtype),
        scratch_shapes=[pltpu.SemaphoreType.DMA((count,))],
        compiler_params=pltpu.CompilerParams(vmem_limit_bytes=VMEM),
    )(w)


def edge_kernel(tokens, values, out, last_tokens, last_values, arrived):
    lines = pl.ds(tokens.shape[0] - ROWS, ROWS)
    moved([(tokens.at[lines, :], last_tokens), (values.at[lines, :], last_values)], arrived)
    margin, width = out.shape[0], tokens.shape[1]
    out[:, :width] = last_tokens[...].astype(jnp.float32)[ROWS - margin :, :].astype(out.dtype)
    out[:, width:] = last_values[...].astype(jnp.float32)[ROWS - margin :, :].astype(out.dtype)


def columns_of(chip, core, depth):
    return pl.ds(pl.multiple_of((2 * chip + core) * depth, 128), depth)


def project(core, hidden, tail, w, main, edge):
    depth = w.shape[1]
    for chip in range(w.shape[0]):
        some = hidden[:, chip * depth : (chip + 1) * depth]
        main += jnp.dot(some, w[chip], preferred_element_type=jnp.float32)
        some = tail[:, columns_of(chip, core, depth)]
        edge += jnp.dot(some, w[chip], preferred_element_type=jnp.float32)
    return main, edge


def split_lanes(wide):
    high = wide.astype(jnp.bfloat16)
    low = (wide - high.astype(jnp.float32)).astype(jnp.bfloat16)
    return jnp.concatenate([high, low], axis=1)


def three_parts(wide):
    parts = []
    for _ in range(3):
        parts.append(wide.astype(jnp.bfloat16))
        wide = wide - parts[-1].astype(jnp.float32)
    return parts


def logs_of(steps):
    head_count, length = steps.shape
    earlier = lax.broadcasted_iota(jnp.int32, (length, length), 0)
    token = lax.broadcasted_iota(jnp.int32, (length, length), 1)
    upto = jnp.where(earlier <= token, 1.0, 0.0).astype(jnp.bfloat16)
    after = jnp.zeros((head_count, length), jnp.float32)
    for part in reversed(three_parts(steps)):
        after += jnp.dot(part, upto, preferred_element_type=jnp.float32)
    return after, lax.broadcasted_iota(jnp.int32, (head_count, length), 1)


def mixed_inputs(values, edge, taps, extended):
    length, channels = values.shape
    margin = taps.shape[0] - 1
    width = channels // GROUP
    extended[ROWS - margin : ROWS, :] = edge
    extended[ROWS:, :] = values[...].astype(jnp.float32)
    for part in range(GROUP):
        lanes = slice(part * width, (part + 1) * width)
        summed = jnp.zeros((length, width), jnp.float32)
        for offset in range(margin + 1):
            first = ROWS - margin + offset
            summed = (
                summed + taps[offset : offset + 1, lanes] * extended[first : first + length, lanes]
            )
        yield part, (summed * jax.nn.sigmoid(summed)).T


def weighted(mixed, weight):
    heads, length = weight.shape
    mixed = mixed.reshape(heads, mixed.shape[0] // heads, length)
    return split_lanes((mixed * weight[:, None, :]).reshape(-1, length))


def inputs_kernel(
    core,
    hidden,
    w,
    steps,
    values,
    before,
    taps,
    ends,
    end_logs,
    tail,
    total,
    rest,
    extended,
    held,
    steps_held,
    taps_held,
    arrived,
    columns,
    landed,
):
    chips, depth, size = w.shape
    moves = [
        pltpu.make_async_copy(
            hidden.at[:, columns_of(chip, side, depth)],
            to.at[:, pl.ds(chip * depth, depth)],
            landed.at[i * chips + chip],
        )
        for i, (side, to) in enumerate(((core[0], columns), (1 - core[0], rest)))
        for chip in range(chips)
    ]
    for move in moves:
        move.start()
    moved([(values, held), (steps, steps_held), (taps, taps_held)], arrived)
    margin = taps.shape[0] - 1
    width = tail.shape[1]
    edge = before[...].astype(jnp.float32)
    zeros = jnp.zeros((ROWS - margin, width), jnp.float32)
    tail[...] = jnp.concatenate([zeros, edge[:, :width]], axis=0).astype(jnp.bfloat16)
    after, token = logs_of(steps_held[...])
    end_log = jnp.sum(jnp.where(token == token.shape[1] - 1, after, 0.0), axis=1, keepdims=True)
    weight = jnp.exp(end_log - after)
    end_logs[...] = jnp.broadcast_to(end_log, end_logs.shape)
    heads = weight.shape[0] // GROUP
    for part, mixed in mixed_inputs(held, edge[:, width:], taps_held, extended):
        rows = mixed.shape[0]
        some = weight[part * heads : (part + 1) * heads, :]
        ends[part * rows : (part + 1) * rows, :] = weighted(mixed, some)
    for move in moves:
        move.wait()
    main = jnp.zeros((hidden.shape[0], size), jnp.float32)
    edge = jnp.zeros((tail.shape[0], size), jnp.float32)
    main, edge = project(core[0], columns, tail, w, main, edge)
    total[0:ROWS, :] = edge
    total[ROWS:, :] = main


def right_side(mixed_b):
    high = mixed_b.astype(jnp.bfloat16)
    low = (mixed_b - high.astype(jnp.float32)).astype(jnp.bfloat16)
    return jnp.concatenate(
        [
            jnp.concatenate([high, low], axis=1),
            jnp.concatenate([high, jnp.zeros_like(low)], axis=1),
        ],
        axis=0,
    )


def state_of(sides, right):
    both = jnp.dot(sides, right, preferred_element_type=jnp.float32)
    size = both.shape[1] // 2
    return both[:, :size] + both[:, size:]


def write_slice(sent, states, logs=None):
    heads, headdim, size = states.shape
    rows = heads * headdim // 2
    scale = scale_codes(jnp.max(jnp.abs(states), axis=1))
    sent[0:rows, :] = words_of(states * up(scale)[:, None, :]).reshape(rows, size)
    notes = scale.astype(jnp.int32)
    sent[rows:, :] = pack(notes, jnp.zeros_like(notes) if logs is None else code_logs(logs))


def read_slice(got, headdim):
    size = got.shape[1]
    half = headdim // 2
    heads = got.shape[0] // (half + 1)
    rows = heads * half
    notes = got[rows:, :]
    states = codes_of(got[0:rows, :].reshape(heads, half, size))
    return states * down(high_of(notes).astype(jnp.float32))[:, None, :], notes


def full_kernel(headdim, core, hidden, tail, w, taps, begun, ends, logs, sent, sides, extended):
    main, edge = project(1 - core[0], hidden, tail, w, begun[ROWS:, :], begun[0:ROWS, :])
    extended[0:ROWS, :] = edge
    extended[ROWS:, :] = main
    kernel = taps.shape[0]
    length, size = main.shape
    summed = jnp.zeros((length, size), jnp.float32)
    for offset in range(kernel):
        first = ROWS - kernel + 1 + offset
        summed = summed + taps[offset : offset + 1, :] * extended[first : first + length, :]
    right = right_side(summed * jax.nn.sigmoid(summed))
    sides[...] = right
    rows = ends.shape[0] // GROUP
    heads = rows // headdim
    for owner in range(GROUP):
        state = state_of(ends[owner * rows : (owner + 1) * rows, :], right)
        write_slice(
            sent.at[owner],
            state.reshape(heads, headdim, size),
            logs[owner * heads : (owner + 1) * heads, :],
        )


def kept_kernel(
    accepted, steps, values, before, taps, right, out, decay, extended, held, steps_held, taps_held, arrived
):
    moved([(values, held), (steps, steps_held), (taps, taps_held)], arrived)
    kept = accepted[0]
    after, token = logs_of(steps_held[...])
    kept_log = jnp.sum(jnp.where(token == kept - 1, after, 0.0), axis=1, keepdims=True)
    inside = token < kept
    weight = jnp.where(inside, jnp.exp(jnp.where(inside, kept_log - after, 0.0)), 0.0)
    decay[...] = jnp.broadcast_to(jnp.exp(kept_log), decay.shape)
    edge = before[...].astype(jnp.float32)[:, before.shape[1] - values.shape[1] :]
    heads = weight.shape[0] // GROUP
    for part, mixed in mixed_inputs(held, edge, taps_held, extended):
        rows = mixed.shape[0]
        some = weight[part * heads : (part + 1) * heads, :]
        out[part * rows : (part + 1) * rows, :] = state_of(weighted(mixed, some), right[...])


def group_kernel(headdim, wraps, got, prefix, decay, sent):
    goes_on = jnp.where(wraps[0] > 0, 0.0, 1.0)
    rows, size = prefix.shape[1:]
    heads = rows // headdim
    half = headdim // 2
    message = half + 1
    carried = jnp.zeros((heads, headdim, size), jnp.float32)
    passed = jnp.zeros((heads, size), jnp.float32)
    for shard in range(GROUP):
        if shard == SHIFT:
            carried = carried * goes_on
            passed = passed * goes_on
        prefix[shard] = carried.reshape(rows, size)
        decay[shard] = jnp.exp(passed) * (goes_on if shard >= SHIFT else 1.0)
        state, notes = read_slice(got.at[shard], headdim)
        log = jnp.broadcast_to(read_logs(notes), (heads, size))
        carried = jnp.exp(log)[:, None, :] * carried + state
        passed = passed + log
    scale = scale_codes(jnp.max(jnp.abs(carried), axis=1))
    words = words_of(carried * up(scale)[:, None, :])
    for head in range(heads):
        sent[head * message + 1 : (head + 1) * message, :] = words[head]
    sent[pl.ds(0, heads, stride=message), :] = pack(scale.astype(jnp.int32), code_logs(passed))


def members_of(groups):
    rows = groups // GROUP
    places = [(place + GROUP // 2) % GROUP for place in range(GROUP)]
    return [row * GROUP + place for place in places for row in reversed(range(rows))]


def scan_kernel(headdim, core, got, sent, held, tops, factors, decays):
    half = headdim // 2
    message = half + 1
    groups = got.shape[0] // message
    size = got.shape[1]
    notes = got[pl.ds(0, groups, stride=message), :]
    factors[...] = down(high_of(notes).astype(jnp.float32))
    decays[...] = jnp.broadcast_to(jnp.exp(read_logs(notes)), decays.shape)
    listed = members_of(groups)
    last = listed.index(groups - 1)
    opening = codes_of(got[last * message + 1 : (last + 1) * message, :])
    carried = opening * factors[last : last + 1, :] * jnp.where(core[0] > 0, 1.0, 0.0)
    for group in range(groups):
        slot = listed.index(group)
        held[slot * headdim : (slot + 1) * headdim, :] = carried
        tops[slot : slot + 1, :] = jnp.max(jnp.abs(carried), axis=0, keepdims=True)
        state = codes_of(got[slot * message + 1 : (slot + 1) * message, :])
        state = state * factors[slot : slot + 1, :]
        carried = decays[slot : slot + 1, :] * carried + state
    scale = scale_codes(tops[...])
    sent[pl.ds(0, groups, stride=message), :] = lax.shift_left(scale.astype(jnp.int32), 16)
    factors[...] = up(scale)
    for group in range(groups):
        scaled = held[group * headdim : (group + 1) * headdim, :] * factors[group : group + 1, :]
        sent[group * message + 1 : (group + 1) * message, :] = words_of(scaled)


def incoming_kernel(headdim, got, prefix, decay, sent, held, factors, staged, arrived):
    shards, rows, size = prefix.shape
    heads = rows // headdim
    half = headdim // 2
    message = half + 1
    notes = got[pl.ds(0, heads, stride=message), :]
    factors[...] = down(high_of(notes).astype(jnp.float32))
    for head in range(heads):
        state = codes_of(got[head * message + 1 : (head + 1) * message, :])
        held[head] = state * factors[head : head + 1, :]
    for shard in range(shards):
        local = prefix[shard].reshape(heads, headdim, size)
        write_slice(staged.at[shard], decay[shard][:, None, :] * held[...] + local)
        pltpu.make_async_copy(staged.at[shard], sent.at[shard], arrived.at[shard]).start()
    for shard in range(shards):
        pltpu.make_async_copy(staged.at[shard], sent.at[shard], arrived.at[shard]).wait()


def final_kernel(headdim, got, kept, part, out, staged, arrived):
    rows = part.shape[0] // GROUP
    size = part.shape[1]
    heads = rows // headdim
    moves = []
    for owner in range(GROUP):
        state, _ = read_slice(got.at[owner], headdim)
        scaled = kept[owner * heads : (owner + 1) * heads, :][:, None, :] * state
        lines = slice(owner * rows, (owner + 1) * rows)
        staged[lines, :] = scaled.reshape(rows, size) + part[lines, :]
        lines = pl.ds(owner * rows, rows)
        moves.append(
            pltpu.make_async_copy(staged.at[lines, :], out.at[lines, :], arrived.at[owner])
        )
        moves[-1].start()
    for move in moves:
        move.wait()


def on_device(hidden, inputs, w_b, conv_x, conv_b, log_decay, accepted):
    tokens = hidden[0]
    values = inputs[0]
    length, width = tokens.shape
    channels = values.shape[1]
    margin = conv_x.shape[0] - 1
    head_count = log_decay.shape[2]
    headdim = channels // head_count
    size = w_b.shape[1]
    message = headdim // 2 + 1
    heads = head_count // GROUP
    rows = heads * headdim
    f32, bf16, i32 = jnp.float32, jnp.bfloat16, jnp.int32
    array = jax.ShapeDtypeStruct
    shards = lax.axis_size("seq")
    parts = lax.axis_size("fsdp")
    group_count = shards // GROUP

    def device(side, part, place):
        return (place + SHIFT * side) % shards * parts + 2 * part + side

    sides = [(side, part) for part in range(parts // 2) for side in range(2)]
    near = [
        [device(side, part, group * GROUP + i) for i in range(GROUP)]
        for side, part in sides
        for group in range(group_count)
    ]
    far = [
        [device(side, part, group * GROUP + i) for group in members_of(group_count)]
        for side, part in sides
        for i in range(GROUP)
    ]
    core = lax.axis_index("fsdp") % 2
    place = (lax.axis_index("seq") - SHIFT * core) % shards
    wraps = jnp.reshape(core * (place // GROUP == group_count - 1), (1,)).astype(i32)
    core = jnp.reshape(core, (1,)).astype(i32)

    def exchange(sent, members):
        return lax.all_to_all(sent, ("seq", "fsdp"), 0, 0, axis_index_groups=members)

    def exchange_heads(sent):
        return exchange(sent.reshape(heads, 1, message * size), far).reshape(sent.shape)

    chips = [[i for i in range(parts) if i % 2 == c] for c in range(2)]
    w_copies = copies(w_b, parts // 2)
    w_own = lax.all_to_all(w_copies, "fsdp", 0, 0, axis_index_groups=chips)
    dma = pltpu.SemaphoreType.DMA
    edge = call(
        edge_kernel,
        tokens,
        values,
        far=(0, 1),
        out=array((margin, width + channels), bf16),
        scratch=[pltpu.VMEM((ROWS, width), bf16), pltpu.VMEM((ROWS, channels), bf16), dma((2,))],
    )
    before = lax.ppermute(edge, "seq", [(i, i + 1) for i in range(shards - 1)])

    steps = log_decay[0].T
    wide = array((head_count, size), f32)
    scratch = [
        pltpu.VMEM((ROWS + length, channels), f32),
        pltpu.VMEM(values.shape, values.dtype),
        pltpu.VMEM(steps.shape, f32),
        pltpu.VMEM(conv_x.shape, f32),
        dma((3,)),
    ]
    w_own, before, core, wraps = lax.optimization_barrier((w_own, before, core, wraps))
    w_other = lax.ppermute(w_own, "fsdp", [(i, i ^ 1) for i in range(parts)])
    ends_x, end_logs, tail, begun, rest = call(
        inputs_kernel,
        core,
        tokens,
        w_own,
        steps,
        values,
        before,
        conv_x,
        far=(1, 3, 4, 6),
        out=[
            array((channels, 2 * length), bf16),
            wide,
            array((ROWS, width), bf16),
            array((ROWS + length, size), f32),
            array((length, width // 2), bf16),
        ],
        scratch=scratch + [pltpu.VMEM((length, width // 2), bf16), dma((parts,))],
    )

    slices = array((GROUP, heads * message, size), i32)
    sent, right = call(
        functools.partial(full_kernel, headdim),
        core,
        rest,
        tail,
        w_other,
        conv_b,
        begun,
        ends_x,
        end_logs,
        out=[slices, array((2 * length, 2 * size), bf16)],
        scratch=[pltpu.VMEM((ROWS + length, size), f32)],
    )
    prefix, decay, sent = call(
        functools.partial(group_kernel, headdim),
        wraps,
        exchange(sent, near),
        out=[
            array((GROUP, rows, size), f32),
            array((GROUP, heads, size), f32),
            array((heads * message, size), i32),
        ],
    )
    part, kept_decay = call(
        kept_kernel,
        accepted[0],
        steps,
        values,
        before,
        conv_x,
        right,
        far=(1, 2, 4),
        out=[array((channels, size), f32), wide],
        scratch=scratch,
    )

    sent = call(
        functools.partial(scan_kernel, headdim),
        core,
        exchange_heads(sent),
        out=array(sent.shape, i32),
        scratch=[pltpu.VMEM((group_count * headdim, size), f32)]
        + [pltpu.VMEM((group_count, size), f32)] * 3,
    )
    sent = call(
        functools.partial(incoming_kernel, headdim),
        exchange_heads(sent),
        prefix,
        decay,
        out=slices,
        out_space=pltpu.HBM,
        scratch=[
            pltpu.VMEM((heads, headdim, size), f32),
            pltpu.VMEM((heads, size), f32),
            pltpu.VMEM(slices.shape, i32),
            dma((GROUP,)),
        ],
    )
    final = call(
        functools.partial(final_kernel, headdim),
        exchange(sent, near),
        kept_decay,
        part,
        out=array((channels, size), f32),
        out_space=pltpu.HBM,
        scratch=[pltpu.VMEM((channels, size), f32), dma((GROUP,))],
    )
    return final.reshape(1, 1, head_count, headdim, size)


def solution(mesh):
    placed = (
        P("fsdp", "seq", None),
        P("fsdp", "seq", None),
        P("fsdp", None),
        P(),
        P(),
        P("fsdp", "seq", None),
        P("fsdp", "seq"),
    )
    return jax.shard_map(
        on_device,
        mesh=mesh,
        in_specs=placed,
        out_specs=P("fsdp", "seq", None, None, None),
        check_vma=False,
    )
```

```python
import functools

import jax
import jax.numpy as jnp
from jax import lax
from jax.experimental import pallas as pl
from jax.experimental.pallas import tpu as pltpu
from jax.sharding import PartitionSpec as P

ROWS = 16
GROUP = 4
SHIFT = 2
TOP = 32760.0
FINE = 128.0
LOG_STEP = float(2**19)
VMEM = 12 * 1024 * 1024


def call(kernel, *args, out, scratch=(), far=(), out_space=pltpu.VMEM):
    places = [
        pltpu.SMEM if a.shape == (1,) else pltpu.HBM if i in far else pltpu.VMEM
        for i, a in enumerate(args)
    ]
    return pl.pallas_call(
        kernel,
        in_specs=[pl.BlockSpec(memory_space=place) for place in places],
        out_specs=jax.tree.map(lambda _: pl.BlockSpec(memory_space=out_space), out),
        out_shape=out,
        scratch_shapes=scratch,
        compiler_params=pltpu.CompilerParams(vmem_limit_bytes=VMEM),
    )(*args)


def scale_codes(top):
    return jnp.ceil(jnp.log2(jnp.maximum(top, 1e-33)) * FINE)


def up(scale):
    return TOP * jnp.exp2(scale * (-1.0 / FINE))


def down(scale):
    return jnp.exp2(scale * (1.0 / FINE)) * (1.0 / TOP)


def pack(high, low):
    return lax.shift_left(high, 16) | (low & 0xFFFF)


def high_of(words):
    return lax.shift_right_arithmetic(words, 16)


def low_of(words):
    return lax.shift_right_arithmetic(lax.shift_left(words, 16), 16)


def words_of(scaled):
    codes = jnp.round(scaled).astype(jnp.int32)
    half = codes.shape[-2] // 2
    return pack(codes[..., :half, :], codes[..., half:, :])


def codes_of(words):
    return jnp.concatenate([high_of(words), low_of(words)], axis=-2).astype(jnp.float32)


def code_logs(logs):
    whole = jnp.round(logs * -LOG_STEP).astype(jnp.int32)
    lane = lax.broadcasted_iota(jnp.int32, logs.shape, 1)
    high = lax.shift_right_logical(whole, 15)
    return jnp.where(lane < logs.shape[1] // 2, high, whole & 0x7FFF)


def read_logs(notes):
    lane = lax.broadcasted_iota(jnp.int32, notes.shape, 1)
    parts = (notes & 0xFFFF).astype(jnp.float32)
    high = jnp.sum(jnp.where(lane == 0, parts, 0.0), axis=1, keepdims=True)
    low = jnp.sum(jnp.where(lane == notes.shape[1] - 1, parts, 0.0), axis=1, keepdims=True)
    return (high * 32768.0 + low) * (-1.0 / LOG_STEP)


def moved(pairs, arrived):
    moves = [
        pltpu.make_async_copy(source, target, arrived.at[i])
        for i, (source, target) in enumerate(pairs)
    ]
    for move in moves:
        move.start()
    for move in moves:
        move.wait()


def copies_kernel(w, out, arrived):
    moved([(w, out.at[copy]) for copy in range(out.shape[0])], arrived)


def copies(w, count):
    return pl.pallas_call(
        copies_kernel,
        in_specs=[pl.BlockSpec(memory_space=pltpu.VMEM)],
        out_specs=pl.BlockSpec(memory_space=pltpu.HBM),
        out_shape=jax.ShapeDtypeStruct((count, *w.shape), w.dtype),
        scratch_shapes=[pltpu.SemaphoreType.DMA((count,))],
        compiler_params=pltpu.CompilerParams(vmem_limit_bytes=VMEM),
    )(w)


def edge_kernel(tokens, values, out, last_tokens, last_values, arrived):
    lines = pl.ds(tokens.shape[0] - ROWS, ROWS)
    moved([(tokens.at[lines, :], last_tokens), (values.at[lines, :], last_values)], arrived)
    margin, width = out.shape[0], tokens.shape[1]
    out[:, :width] = last_tokens[...].astype(jnp.float32)[ROWS - margin :, :].astype(out.dtype)
    out[:, width:] = last_values[...].astype(jnp.float32)[ROWS - margin :, :].astype(out.dtype)


def columns_of(chip, core, depth):
    return pl.ds(pl.multiple_of((2 * chip + core) * depth, 128), depth)


def project(core, hidden, tail, w, main, edge):
    depth = w.shape[1]
    for chip in range(w.shape[0]):
        some = hidden[:, chip * depth : (chip + 1) * depth]
        main += jnp.dot(some, w[chip], preferred_element_type=jnp.float32)
        some = tail[:, columns_of(chip, core, depth)]
        edge += jnp.dot(some, w[chip], preferred_element_type=jnp.float32)
    return main, edge


def partial_kernel(core, hidden, tail, w, total, rest, held, arrived):
    chips, depth, size = w.shape
    moved(
        [
            (hidden.at[:, columns_of(chip, side, depth)], to.at[:, pl.ds(chip * depth, depth)])
            for side, to in ((core[0], held), (1 - core[0], rest))
            for chip in range(chips)
        ],
        arrived,
    )
    main = jnp.zeros((hidden.shape[0], size), jnp.float32)
    edge = jnp.zeros((tail.shape[0], size), jnp.float32)
    main, edge = project(core[0], held, tail, w, main, edge)
    total[0:ROWS, :] = edge
    total[ROWS:, :] = main


def split_lanes(wide):
    high = wide.astype(jnp.bfloat16)
    low = (wide - high.astype(jnp.float32)).astype(jnp.bfloat16)
    return jnp.concatenate([high, low], axis=1)


def three_parts(wide):
    parts = []
    for _ in range(3):
        parts.append(wide.astype(jnp.bfloat16))
        wide = wide - parts[-1].astype(jnp.float32)
    return parts


def logs_of(steps):
    head_count, length = steps.shape
    earlier = lax.broadcasted_iota(jnp.int32, (length, length), 0)
    token = lax.broadcasted_iota(jnp.int32, (length, length), 1)
    upto = jnp.where(earlier <= token, 1.0, 0.0).astype(jnp.bfloat16)
    after = jnp.zeros((head_count, length), jnp.float32)
    for part in reversed(three_parts(steps)):
        after += jnp.dot(part, upto, preferred_element_type=jnp.float32)
    return after, lax.broadcasted_iota(jnp.int32, (head_count, length), 1)


def mixed_inputs(values, edge, taps, extended):
    length, channels = values.shape
    margin = taps.shape[0] - 1
    width = channels // GROUP
    extended[ROWS - margin : ROWS, :] = edge
    extended[ROWS:, :] = values[...].astype(jnp.float32)
    for part in range(GROUP):
        lanes = slice(part * width, (part + 1) * width)
        summed = jnp.zeros((length, width), jnp.float32)
        for offset in range(margin + 1):
            first = ROWS - margin + offset
            summed = (
                summed + taps[offset : offset + 1, lanes] * extended[first : first + length, lanes]
            )
        yield part, (summed * jax.nn.sigmoid(summed)).T


def weighted(mixed, weight):
    heads, length = weight.shape
    mixed = mixed.reshape(heads, mixed.shape[0] // heads, length)
    return split_lanes((mixed * weight[:, None, :]).reshape(-1, length))


def inputs_kernel(
    steps, values, before, taps, ends, end_logs, tail, extended, held, steps_held, taps_held, arrived
):
    moved([(values, held), (steps, steps_held), (taps, taps_held)], arrived)
    margin = taps.shape[0] - 1
    width = tail.shape[1]
    edge = before[...].astype(jnp.float32)
    zeros = jnp.zeros((ROWS - margin, width), jnp.float32)
    tail[...] = jnp.concatenate([zeros, edge[:, :width]], axis=0).astype(jnp.bfloat16)
    after, token = logs_of(steps_held[...])
    end_log = jnp.sum(jnp.where(token == token.shape[1] - 1, after, 0.0), axis=1, keepdims=True)
    weight = jnp.exp(end_log - after)
    end_logs[...] = jnp.broadcast_to(end_log, end_logs.shape)
    heads = weight.shape[0] // GROUP
    for part, mixed in mixed_inputs(held, edge[:, width:], taps_held, extended):
        rows = mixed.shape[0]
        some = weight[part * heads : (part + 1) * heads, :]
        ends[part * rows : (part + 1) * rows, :] = weighted(mixed, some)


def right_side(mixed_b):
    high = mixed_b.astype(jnp.bfloat16)
    low = (mixed_b - high.astype(jnp.float32)).astype(jnp.bfloat16)
    return jnp.concatenate(
        [
            jnp.concatenate([high, low], axis=1),
            jnp.concatenate([high, jnp.zeros_like(low)], axis=1),
        ],
        axis=0,
    )


def state_of(sides, right):
    both = jnp.dot(sides, right, preferred_element_type=jnp.float32)
    size = both.shape[1] // 2
    return both[:, :size] + both[:, size:]


def write_slice(sent, states, logs=None):
    heads, headdim, size = states.shape
    rows = heads * headdim // 2
    scale = scale_codes(jnp.max(jnp.abs(states), axis=1))
    sent[0:rows, :] = words_of(states * up(scale)[:, None, :]).reshape(rows, size)
    notes = scale.astype(jnp.int32)
    sent[rows:, :] = pack(notes, jnp.zeros_like(notes) if logs is None else code_logs(logs))


def read_slice(got, headdim):
    size = got.shape[1]
    half = headdim // 2
    heads = got.shape[0] // (half + 1)
    rows = heads * half
    notes = got[rows:, :]
    states = codes_of(got[0:rows, :].reshape(heads, half, size))
    return states * down(high_of(notes).astype(jnp.float32))[:, None, :], notes


def full_kernel(headdim, core, hidden, tail, w, taps, begun, ends, logs, sent, sides, extended):
    main, edge = project(1 - core[0], hidden, tail, w, begun[ROWS:, :], begun[0:ROWS, :])
    extended[0:ROWS, :] = edge
    extended[ROWS:, :] = main
    kernel = taps.shape[0]
    length, size = main.shape
    summed = jnp.zeros((length, size), jnp.float32)
    for offset in range(kernel):
        first = ROWS - kernel + 1 + offset
        summed = summed + taps[offset : offset + 1, :] * extended[first : first + length, :]
    right = right_side(summed * jax.nn.sigmoid(summed))
    sides[...] = right
    rows = ends.shape[0] // GROUP
    heads = rows // headdim
    for owner in range(GROUP):
        state = state_of(ends[owner * rows : (owner + 1) * rows, :], right)
        write_slice(
            sent.at[owner],
            state.reshape(heads, headdim, size),
            logs[owner * heads : (owner + 1) * heads, :],
        )


def kept_kernel(
    accepted, steps, values, before, taps, right, out, decay, extended, held, steps_held, taps_held, arrived
):
    moved([(values, held), (steps, steps_held), (taps, taps_held)], arrived)
    kept = accepted[0]
    after, token = logs_of(steps_held[...])
    kept_log = jnp.sum(jnp.where(token == kept - 1, after, 0.0), axis=1, keepdims=True)
    inside = token < kept
    weight = jnp.where(inside, jnp.exp(jnp.where(inside, kept_log - after, 0.0)), 0.0)
    decay[...] = jnp.broadcast_to(jnp.exp(kept_log), decay.shape)
    edge = before[...].astype(jnp.float32)[:, before.shape[1] - values.shape[1] :]
    heads = weight.shape[0] // GROUP
    for part, mixed in mixed_inputs(held, edge, taps_held, extended):
        rows = mixed.shape[0]
        some = weight[part * heads : (part + 1) * heads, :]
        out[part * rows : (part + 1) * rows, :] = state_of(weighted(mixed, some), right[...])


def group_kernel(headdim, wraps, got, prefix, decay, sent):
    goes_on = jnp.where(wraps[0] > 0, 0.0, 1.0)
    rows, size = prefix.shape[1:]
    heads = rows // headdim
    half = headdim // 2
    message = half + 1
    carried = jnp.zeros((heads, headdim, size), jnp.float32)
    passed = jnp.zeros((heads, size), jnp.float32)
    for shard in range(GROUP):
        if shard == SHIFT:
            carried = carried * goes_on
            passed = passed * goes_on
        prefix[shard] = carried.reshape(rows, size)
        decay[shard] = jnp.exp(passed) * (goes_on if shard >= SHIFT else 1.0)
        state, notes = read_slice(got.at[shard], headdim)
        log = jnp.broadcast_to(read_logs(notes), (heads, size))
        carried = jnp.exp(log)[:, None, :] * carried + state
        passed = passed + log
    scale = scale_codes(jnp.max(jnp.abs(carried), axis=1))
    words = words_of(carried * up(scale)[:, None, :])
    for head in range(heads):
        sent[head * message + 1 : (head + 1) * message, :] = words[head]
    sent[pl.ds(0, heads, stride=message), :] = pack(scale.astype(jnp.int32), code_logs(passed))


def members_of(groups):
    rows = groups // GROUP
    places = [(place + GROUP // 2) % GROUP for place in range(GROUP)]
    return [row * GROUP + place for place in places for row in reversed(range(rows))]


def scan_kernel(headdim, core, got, sent, held, tops, factors, decays):
    half = headdim // 2
    message = half + 1
    groups = got.shape[0] // message
    size = got.shape[1]
    notes = got[pl.ds(0, groups, stride=message), :]
    factors[...] = down(high_of(notes).astype(jnp.float32))
    decays[...] = jnp.broadcast_to(jnp.exp(read_logs(notes)), decays.shape)
    listed = members_of(groups)
    last = listed.index(groups - 1)
    opening = codes_of(got[last * message + 1 : (last + 1) * message, :])
    carried = opening * factors[last : last + 1, :] * jnp.where(core[0] > 0, 1.0, 0.0)
    for group in range(groups):
        slot = listed.index(group)
        held[slot * headdim : (slot + 1) * headdim, :] = carried
        tops[slot : slot + 1, :] = jnp.max(jnp.abs(carried), axis=0, keepdims=True)
        state = codes_of(got[slot * message + 1 : (slot + 1) * message, :])
        state = state * factors[slot : slot + 1, :]
        carried = decays[slot : slot + 1, :] * carried + state
    scale = scale_codes(tops[...])
    sent[pl.ds(0, groups, stride=message), :] = lax.shift_left(scale.astype(jnp.int32), 16)
    factors[...] = up(scale)
    for group in range(groups):
        scaled = held[group * headdim : (group + 1) * headdim, :] * factors[group : group + 1, :]
        sent[group * message + 1 : (group + 1) * message, :] = words_of(scaled)


def incoming_kernel(headdim, got, prefix, decay, sent, held, factors, staged, arrived):
    shards, rows, size = prefix.shape
    heads = rows // headdim
    half = headdim // 2
    message = half + 1
    notes = got[pl.ds(0, heads, stride=message), :]
    factors[...] = down(high_of(notes).astype(jnp.float32))
    for head in range(heads):
        state = codes_of(got[head * message + 1 : (head + 1) * message, :])
        held[head] = state * factors[head : head + 1, :]
    for shard in range(shards):
        local = prefix[shard].reshape(heads, headdim, size)
        write_slice(staged.at[shard], decay[shard][:, None, :] * held[...] + local)
        pltpu.make_async_copy(staged.at[shard], sent.at[shard], arrived.at[shard]).start()
    for shard in range(shards):
        pltpu.make_async_copy(staged.at[shard], sent.at[shard], arrived.at[shard]).wait()


def final_kernel(headdim, got, kept, part, out, staged, arrived):
    words = headdim // 2
    heads = got.shape[1] // (words + 1)
    few = heads // 2
    size = part.shape[1]
    moves = []
    for piece in range(2 * GROUP):
        owner, first = piece // 2, piece % 2 * few
        notes = got[owner, heads * words + first : heads * words + first + few, :]
        coded = got[owner, first * words : (first + few) * words, :].reshape(few, words, size)
        factor = down(high_of(notes).astype(jnp.float32)) * kept[piece * few : (piece + 1) * few, :]
        rows = few * headdim
        lines = slice(piece * rows, (piece + 1) * rows)
        staged[lines, :] = (codes_of(coded) * factor[:, None, :]).reshape(rows, size) + part[lines, :]
        lines = pl.ds(piece * rows, rows)
        moves.append(
            pltpu.make_async_copy(staged.at[lines, :], out.at[lines, :], arrived.at[piece])
        )
        moves[-1].start()
    for move in moves:
        move.wait()


def on_device(hidden, inputs, w_b, conv_x, conv_b, log_decay, accepted):
    tokens = hidden[0]
    values = inputs[0]
    length, width = tokens.shape
    channels = values.shape[1]
    margin = conv_x.shape[0] - 1
    head_count = log_decay.shape[2]
    headdim = channels // head_count
    size = w_b.shape[1]
    message = headdim // 2 + 1
    heads = head_count // GROUP
    rows = heads * headdim
    f32, bf16, i32 = jnp.float32, jnp.bfloat16, jnp.int32
    array = jax.ShapeDtypeStruct
    shards = lax.axis_size("seq")
    parts = lax.axis_size("fsdp")
    group_count = shards // GROUP

    def device(side, part, place):
        return (place + SHIFT * side) % shards * parts + 2 * part + side

    sides = [(side, part) for part in range(parts // 2) for side in range(2)]
    near = [
        [device(side, part, group * GROUP + i) for i in range(GROUP)]
        for side, part in sides
        for group in range(group_count)
    ]
    far = [
        [device(side, part, group * GROUP + i) for group in members_of(group_count)]
        for side, part in sides
        for i in range(GROUP)
    ]
    core = lax.axis_index("fsdp") % 2
    place = (lax.axis_index("seq") - SHIFT * core) % shards
    wraps = jnp.reshape(core * (place // GROUP == group_count - 1), (1,)).astype(i32)
    core = jnp.reshape(core, (1,)).astype(i32)

    def exchange(sent, members):
        return lax.all_to_all(sent, ("seq", "fsdp"), 0, 0, axis_index_groups=members)

    def exchange_heads(sent):
        return exchange(sent.reshape(heads, 1, message * size), far).reshape(sent.shape)

    chips = [[i for i in range(parts) if i % 2 == c] for c in range(2)]
    w_copies = copies(w_b, parts // 2)
    w_own = lax.all_to_all(w_copies, "fsdp", 0, 0, axis_index_groups=chips)
    dma = pltpu.SemaphoreType.DMA
    edge = call(
        edge_kernel,
        tokens,
        values,
        far=(0, 1),
        out=array((margin, width + channels), bf16),
        scratch=[pltpu.VMEM((ROWS, width), bf16), pltpu.VMEM((ROWS, channels), bf16), dma((2,))],
    )
    before = lax.ppermute(edge, "seq", [(i, i + 1) for i in range(shards - 1)])

    steps = log_decay[0].T
    wide = array((head_count, size), f32)
    scratch = [
        pltpu.VMEM((ROWS + length, channels), f32),
        pltpu.VMEM(values.shape, values.dtype),
        pltpu.VMEM(steps.shape, f32),
        pltpu.VMEM(conv_x.shape, f32),
        dma((3,)),
    ]
    ends_x, end_logs, tail = call(
        inputs_kernel,
        steps,
        values,
        before,
        conv_x,
        far=(0, 1, 3),
        out=[array((channels, 2 * length), bf16), wide, array((ROWS, width), bf16)],
        scratch=scratch,
    )

    w_own, before, core, wraps = lax.optimization_barrier((w_own, before, core, wraps))
    w_other = lax.ppermute(w_own, "fsdp", [(i, i ^ 1) for i in range(parts)])
    begun, rest = call(
        partial_kernel,
        core,
        tokens,
        tail,
        w_own,
        far=(1,),
        out=[array((ROWS + length, size), f32), array((length, width // 2), bf16)],
        scratch=[pltpu.VMEM((length, width // 2), bf16), dma((parts,))],
    )

    slices = array((GROUP, heads * message, size), i32)
    sent, right = call(
        functools.partial(full_kernel, headdim),
        core,
        rest,
        tail,
        w_other,
        conv_b,
        begun,
        ends_x,
        end_logs,
        out=[slices, array((2 * length, 2 * size), bf16)],
        scratch=[pltpu.VMEM((ROWS + length, size), f32)],
    )
    prefix, decay, sent = call(
        functools.partial(group_kernel, headdim),
        wraps,
        exchange(sent, near),
        out=[
            array((GROUP, rows, size), f32),
            array((GROUP, heads, size), f32),
            array((heads * message, size), i32),
        ],
    )
    part, kept_decay = call(
        kept_kernel,
        accepted[0],
        steps,
        values,
        before,
        conv_x,
        right,
        far=(1, 2, 4),
        out=[array((channels, size), f32), wide],
        scratch=scratch,
    )

    sent = call(
        functools.partial(scan_kernel, headdim),
        core,
        exchange_heads(sent),
        out=array(sent.shape, i32),
        scratch=[pltpu.VMEM((group_count * headdim, size), f32)]
        + [pltpu.VMEM((group_count, size), f32)] * 3,
    )
    sent = call(
        functools.partial(incoming_kernel, headdim),
        exchange_heads(sent),
        prefix,
        decay,
        out=slices,
        out_space=pltpu.HBM,
        scratch=[
            pltpu.VMEM((heads, headdim, size), f32),
            pltpu.VMEM((heads, size), f32),
            pltpu.VMEM(slices.shape, i32),
            dma((GROUP,)),
        ],
    )
    final = call(
        functools.partial(final_kernel, headdim),
        exchange(sent, near),
        kept_decay,
        part,
        out=array((channels, size), f32),
        out_space=pltpu.HBM,
        scratch=[pltpu.VMEM((channels, size), f32), dma((2 * GROUP,))],
    )
    return final.reshape(1, 1, head_count, headdim, size)


def solution(mesh):
    placed = (
        P("fsdp", "seq", None),
        P("fsdp", "seq", None),
        P("fsdp", None),
        P(),
        P(),
        P("fsdp", "seq", None),
        P("fsdp", "seq"),
    )
    return jax.shard_map(
        on_device,
        mesh=mesh,
        in_specs=placed,
        out_specs=P("fsdp", "seq", None, None, None),
        check_vma=False,
    )
```
